32 devices in a mesh: dp: 16 (over z, y, core), rows: 2 (over x).
Axes of the slice: x: 2, y: 2, z: 4, core: 2. Of those that a mesh axis runs over, the one named last changes fastest.
Arguments:
- latents: bfloat16 [16, 32, 32, 640], P('dp', 'rows'), may hold values from -6 to 6
- target: bfloat16 [16, 32, 32, 640], P('dp', 'rows'), may hold values from -6 to 6
- weight: float32 [9, 640, 640], P(None, 'rows', 'dp'), may hold values from -0.078125 to 0.078125
- moment1: float32 [9, 640, 640], P(None, 'rows', 'dp'), may hold values from -6 to 6
- moment2: float32 [9, 640, 640], P(None, 'rows', 'dp'), may hold values from 0.5 to 4
Outputs:
- student: bfloat16 [16, 32, 32, 640], P('dp', 'rows')
- input_grad: bfloat16 [16, 32, 32, 640], P('dp', 'rows')
- new_weight: float32 [9, 640, 640], P(None, 'rows', 'dp')
- new_moment1: float32 [9, 640, 640], P(None, 'rows', 'dp')
- new_moment2: float32 [9, 640, 640], P(None, 'rows', 'dp')
The draws below stay inside these ranges and needn't reach their ends.
All inputs are finite; a program needn't handle non-finite values.
Results may differ from the reference program's by a relative error of at most 0.009.
Values may be sent and summed in bfloat16 or wider, within the bound.
No kernel may reach another device: no remote copies, remote signals or barrier semaphores. Data moves between devices by JAX's collectives and lax.ppermute only.
A program may use at most 128 MiB of HBM per device.

```python
import math
import jax
import jax.numpy as jnp
from jax import lax

CH = 640
HEIGHT = 32
WIDTH = 32
B_DEV = 1
BATCH = 16
N_DP = 16
N_ROWS = 2


def shard_levels(own_key, shape, shards, low, largest):
    gain = 1.0
    for axis_at, parts in shards:
        steps = jax.random.uniform(jax.random.fold_in(jax.random.fold_in(own_key, 6), axis_at), (parts,), jnp.float32, low / len(shards), largest / len(shards))
        gain = gain * jnp.repeat(jnp.exp(steps), shape[axis_at] // parts).reshape((-1,) + (1,) * (len(shape) - 1 - axis_at))
    return gain


def scatter_about(rng, extent, deviation, reach, split=(), kind=jnp.bfloat16):
    result = deviation * jax.random.normal(rng, extent, jnp.float32)
    if split:
        result = result * shard_levels(rng, extent, split, -0.22, 0.18)
    return jnp.clip(result, -reach, reach).astype(kind)


def setup_inputs(seed: int = 0) -> dict:
    streams_of = jax.random.split(jax.random.key(seed), 6)
    return {
        "latents": scatter_about(streams_of[0], (BATCH, HEIGHT, WIDTH, CH), 1.0, 6.0, ((0, 16), (1, 2))),
        "target": scatter_about(streams_of[1], (BATCH, HEIGHT, WIDTH, CH), 1.0, 6.0, ((0, 16), (1, 2))),
        "weight": scatter_about(streams_of[2], (9, CH, CH), (9 * CH) ** -0.5, 0.078125, ((1, 2), (2, 16)), jnp.float32),
        "moment1": scatter_about(streams_of[3], (9, CH, CH), 1.0, 6.0, ((1, 2), (2, 16)), jnp.float32),
        "moment2": jnp.clip(jnp.exp(math.log(4.0) - 2.0794415 * jax.random.uniform(streams_of[4], (9, CH, CH), jnp.float32) ** shard_levels(streams_of[4], (9, CH, CH), ((1, 2), (2, 16)), -0.2, 0.2)), 0.5, 4.0),
    }


def forward_conv(padded, kernel):
    total = jnp.zeros(padded.shape[:1] + (HEIGHT, WIDTH, CH), jnp.float32)
    for tap in range(9):
        a, c = divmod(tap, 3)
        window = padded[:, a:a + HEIGHT, c:c + WIDTH].astype(jnp.float32)
        total = total + jnp.einsum('bhwc,cn->bhwn', window, kernel[tap].astype(jnp.float32))
    return total

def backward_conv(error_pad, kernel):
    total = jnp.zeros(error_pad.shape[:1] + (HEIGHT, WIDTH, CH), jnp.float32)
    for tap in range(9):
        a, c = divmod(tap, 3)
        window = error_pad[:, 2 - a:2 - a + HEIGHT, 2 - c:2 - c + WIDTH].astype(jnp.float32)
        total = total + jnp.einsum('bhwn,cn->bhwc', window, kernel[tap].astype(jnp.float32))
    return total

def reference(latents, target, weight, moment1, moment2):
    kernel = weight.astype(jnp.bfloat16)
    pad_spec = ((0, 0), (1, 1), (1, 1), (0, 0))
    padded = jnp.pad(latents, pad_spec)
    student = forward_conv(padded, kernel).astype(jnp.bfloat16)
    error = (student.astype(jnp.float32) - target.astype(jnp.float32)).astype(jnp.bfloat16)
    error_pad = jnp.pad(error, pad_spec)
    input_grad = backward_conv(error_pad, kernel).astype(jnp.bfloat16)
    band = HEIGHT // N_ROWS

    def group_step(total, group):
        start = (group * B_DEV).astype(jnp.int32)
        xs = lax.dynamic_slice_in_dim(padded, start, B_DEV, 0)
        es = lax.dynamic_slice_in_dim(error, start, B_DEV, 0).astype(jnp.float32)
        es = es.reshape(B_DEV, N_ROWS, band, WIDTH, CH)
        pieces = []
        for tap in range(9):
            a, c = divmod(tap, 3)
            window = xs[:, a:a + HEIGHT, c:c + WIDTH].astype(jnp.float32)
            window = window.reshape(B_DEV, N_ROWS, band, WIDTH, CH)
            part = jnp.einsum('bkhwc,bkhwn->kcn', window, es)
            part = part.astype(jnp.bfloat16).astype(jnp.float32)
            pieces.append(lax.optimization_barrier(jnp.sum(part, axis=0)))
        return (total + jnp.stack(pieces), None)
    summed, _ = lax.scan(group_step, jnp.zeros((9, CH, CH), jnp.float32), jnp.arange(N_DP, dtype=jnp.int32))
    grad = summed / jnp.float32(BATCH)
    new_moment1 = 0.9 * moment1 + 0.1 * grad
    new_moment2 = 0.999 * moment2 + 0.001 * grad * grad
    new_weight = weight - 0.01 * new_moment1 / (jnp.sqrt(new_moment2) + 1e-08)
    return (student, input_grad, new_weight, new_moment1, new_moment2)
```

```python
import functools

import jax
import jax.numpy as jnp
import numpy as np
from jax import lax
from jax.experimental import pallas as pl
from jax.experimental.pallas import tpu as pltpu
from jax.sharding import PartitionSpec as P

BF = jnp.bfloat16
F32 = jnp.float32
NT = (((1,), (1,)), ((), ()))
NN = (((1,), (0,)), ((), ()))
VMEM_LIMIT = 48 << 20
TAPS = 9
ROUTES = (8, 16, 16)


def mm(a, b, dims):
    return lax.dot_general(a, b, dims, preferred_element_type=F32)


def conv_student(kernel_ref, x_ref, t_ref, s_ref, e_ref, width):
    wide = x_ref.shape[2]
    cells = x_ref.shape[1] - 2 * width
    for l in range(x_ref.shape[0]):
        at = slice(l * cells, (l + 1) * cells)
        total = None
        for a in range(3):
            term = mm(
                kernel_ref[:, a * wide : (a + 1) * wide],
                x_ref[l, a * width : a * width + cells, :],
                NT,
            )
            total = term if total is None else total + term
        student = total.astype(BF)
        s_ref[:, at] = student
        e_ref[:, at] = (student.astype(F32) - t_ref[:, at].astype(F32)).astype(BF)


def tap_grad(x_ref, e_ref, tap, width):
    a, c = divmod(tap, 3)
    channels = x_ref.shape[2] // 3
    cells = x_ref.shape[1] - 2 * width
    total = None
    for l in range(x_ref.shape[0]):
        term = mm(
            e_ref[:, l * cells : (l + 1) * cells],
            x_ref[l, a * width : a * width + cells, c * channels : (c + 1) * channels],
            NN,
        )
        total = term if total is None else total + term
    return total


def plain_kernel(width, kernel_ref, x_ref, t_ref, s_ref, e_ref, g_ref):
    channels = x_ref.shape[2] // 3
    conv_student(kernel_ref, x_ref, t_ref, s_ref, e_ref, width)
    for tap in range(TAPS):
        g_ref[:, tap * channels : (tap + 1) * channels] = tap_grad(
            x_ref, e_ref, tap, width
        ).astype(BF)


def routed_kernel(width, half_ref, w_ref, x_ref, t_ref, k_ref, s_ref, e_ref, *outs):
    a_refs, (b0_ref, b1_ref, c0_ref, c1_ref, mid_ref) = outs[:4], outs[4:]
    first = half_ref[0]
    second = 1 - first
    low = lax.broadcasted_iota(jnp.int32, (w_ref.shape[1], 128), 1) < 64
    spare = TAPS * 256
    for tap in range(TAPS):
        k_ref[:, tap * 640 : tap * 640 + 256] = w_ref[first, :, tap * 256 : (tap + 1) * 256]
        k_ref[:, tap * 640 + 384 : (tap + 1) * 640] = w_ref[second, :, tap * 256 : (tap + 1) * 256]
    for pair in range(5):
        at = slice(spare + pair * 128, spare + (pair + 1) * 128)
        left = w_ref[first, :, at].astype(F32)
        right = w_ref[second, :, at].astype(F32)
        k_ref[:, 2 * pair * 640 + 256 : 2 * pair * 640 + 384] = jnp.where(
            low, left, pltpu.roll(right, 64, 1)
        ).astype(BF)
        if 2 * pair + 1 < TAPS:
            k_ref[:, (2 * pair + 1) * 640 + 256 : (2 * pair + 1) * 640 + 384] = jnp.where(
                low, pltpu.roll(left, 64, 1), right
            ).astype(BF)
    conv_student(k_ref, x_ref, t_ref, s_ref, e_ref, width)

    is_first = first == 0

    def put(at, lo, hi):
        own = jnp.where(is_first, lo, hi).astype(BF)
        other = jnp.where(is_first, hi, lo).astype(BF)
        for s in range(4):
            a_refs[s][0, :, at] = own[s * 16 : (s + 1) * 16]
            a_refs[s][1, :, at] = other[s * 16 : (s + 1) * 16]
        b0_ref[0, :, at] = own[64:128]
        b0_ref[1, :, at] = other[64:128]
        b1_ref[0, :, at] = own[128:192]
        b1_ref[1, :, at] = other[128:192]
        c0_ref[:, at] = own[192:]
        c1_ref[:, at] = other[192:]

    for tap in range(TAPS):
        grad = tap_grad(x_ref, e_ref, tap, width)
        put(slice(tap * 256, (tap + 1) * 256), grad[:, :256], grad[:, 384:])
        mid_ref[tap] = grad[:, 256:384]
    for pair in range(5):
        even = mid_ref[2 * pair]
        odd = mid_ref[2 * pair + 1] if 2 * pair + 1 < TAPS else jnp.zeros_like(even)
        put(
            slice(spare + pair * 128, spare + (pair + 1) * 128),
            jnp.where(low, even, pltpu.roll(odd, 64, 1)),
            jnp.where(low, pltpu.roll(even, 64, 1), odd),
        )


def back_kernel(width, kernel_ref, e_ref, out_ref):
    channels = kernel_ref.shape[1] // TAPS
    cells = e_ref.shape[2] - 2 * width
    for l in range(e_ref.shape[1]):
        total = None
        for tap in range(TAPS):
            a, c = divmod(tap, 3)
            term = mm(
                e_ref[c, l, (2 - a) * width : (2 - a) * width + cells, :],
                kernel_ref[:, tap * channels : (tap + 1) * channels],
                NN,
            )
            total = term if total is None else total + term
        out_ref[l] = total


def vmem_call(kernel, outs, scalars, *args, scratch=()):
    flops = 2 * 1024 * 320 * 5760
    return pl.pallas_call(
        kernel,
        out_shape=outs,
        in_specs=[pl.BlockSpec(memory_space=pltpu.SMEM)] * scalars
        + [pl.BlockSpec(memory_space=pltpu.VMEM)] * (len(args) - scalars),
        out_specs=jax.tree.map(lambda _: pl.BlockSpec(memory_space=pltpu.VMEM), outs),
        scratch_shapes=scratch,
        cost_estimate=pl.CostEstimate(flops=flops, bytes_accessed=8 << 20, transcendentals=0),
        compiler_params=pltpu.CompilerParams(vmem_limit_bytes=VMEM_LIMIT),
    )(*args)


def shape(*dims, dtype=BF):
    return jax.ShapeDtypeStruct(dims, dtype)


def column_shift(cells, by):
    if by == 0:
        return cells
    zero = jnp.zeros_like(cells[:, :, :1])
    if by > 0:
        return jnp.concatenate([cells[:, :, 1:], zero], axis=2)
    return jnp.concatenate([zero, cells[:, :, :-1]], axis=2)


def adam(weight, moment1, moment2, grad):
    new_moment1 = 0.9 * moment1 + 0.1 * grad
    new_moment2 = 0.999 * moment2 + 0.001 * grad * grad
    new_weight = weight - 0.01 * new_moment1 / (jnp.sqrt(new_moment2) + 1e-08)
    return new_weight, new_moment1, new_moment2


def with_halo(cells):
    count = lax.axis_size("rows")
    if count == 2:
        at_top = lax.axis_index("rows") == 0
        edge = jnp.where(at_top, cells[:, -1:], cells[:, :1])
        got = lax.ppermute(edge, "rows", [(0, 1), (1, 0)])
        zero = jnp.zeros_like(got)
        return jnp.concatenate(
            [jnp.where(at_top, zero, got), cells, jnp.where(at_top, got, zero)], axis=1
        )
    up = lax.ppermute(cells[:, -1:], "rows", [(i, i + 1) for i in range(count - 1)])
    down = lax.ppermute(cells[:, :1], "rows", [(i + 1, i) for i in range(count - 1)])
    return jnp.concatenate([up, cells, down], axis=1)


def wide_cells(cells):
    b, h, w, c = cells.shape
    return jnp.concatenate([column_shift(cells, k - 1) for k in range(3)], axis=3).reshape(
        b, h * w, 3 * c
    )


def back_cells(error):
    b, h, w, n = error.shape
    return jnp.stack([column_shift(error, 1 - k) for k in range(3)]).reshape(3, b, h * w, n)


def general_device(latents, target, weight, moment1, moment2):
    b, band, width, channels = latents.shape
    cells = b * band * width
    part, outs = weight.shape[1], weight.shape[2]
    row_count = lax.axis_size("rows")
    packed = weight.astype(BF).transpose(2, 0, 1)
    gathered = lax.all_gather(packed, "dp", axis=0, tiled=True)
    kernel = lax.all_gather(gathered, "rows", axis=2, tiled=True)
    total_out = kernel.shape[0]
    kernel = kernel.reshape(total_out, TAPS * channels)
    x = wide_cells(with_halo(latents))
    t = target.reshape(cells, total_out).T
    student, error, grad = vmem_call(
        functools.partial(plain_kernel, width),
        (shape(total_out, cells), shape(total_out, cells), shape(total_out, TAPS * channels)),
        0,
        kernel,
        x,
        t,
    )
    error = error.T.reshape(b, band, width, total_out)
    back = vmem_call(
        functools.partial(back_kernel, width),
        shape(b, band * width, channels, dtype=F32),
        0,
        kernel,
        back_cells(with_halo(error)),
    )
    grad = grad.astype(F32).reshape(total_out, TAPS, row_count, part).transpose(2, 0, 1, 3)
    grad = lax.psum_scatter(grad, "rows", scatter_dimension=0, tiled=True)[0]
    grad = lax.psum_scatter(grad, "dp", scatter_dimension=0, tiled=True)
    grad = grad.transpose(1, 2, 0) / F32(b * lax.axis_size("dp"))
    return (
        student.T.reshape(latents.shape),
        back.astype(BF).reshape(latents.shape),
        *adam(weight, moment1, moment2, grad),
    )


def routed_device(latents, target, weight, moment1, moment2):
    b, band, width, channels = latents.shape
    cells = band * width
    index = lax.axis_index("dp")
    core, y, z = index % 2, (index // 2) % 2, index // 4
    half = lax.axis_index("rows")
    along_core = lambda v: lax.ppermute(v, "dp", [(i, i ^ 1) for i in range(16)])
    along_y = lambda v: lax.ppermute(v, "dp", [(i, i ^ 2) for i in range(16)])
    along_z = lambda v, s: lax.ppermute(v, "dp", [(i, (i + 4 * s) % 16) for i in range(16)])
    along_x = lambda v: lax.ppermute(v, "rows", [(0, 1), (1, 0)])
    ra, rb, rc = ROUTES
    lanes = TAPS * 256 + 640

    piece = weight.transpose(2, 0, 1)
    piece = jnp.where(half == 0, piece, jnp.roll(piece, -64, axis=2)).astype(BF)
    piece = jnp.concatenate(
        [
            piece[:, :, :256].reshape(-1, TAPS * 256),
            piece[:, :, 256:].reshape(-1, TAPS * 64),
            jnp.zeros((piece.shape[0], 64), BF),
        ],
        axis=1,
    )

    pa, pbc = piece[:ra], piece[ra:]
    zbc = jnp.stack([pbc] + [along_z(pbc, s) for s in (1, 2, 3)])
    pa = jnp.stack([pa, along_x(pa)])
    pa = jnp.stack([pa, along_y(pa)], axis=1)
    pb, pc = zbc[:, :rb], zbc[:, rb:]
    pb = jnp.stack([pb, along_x(pb)])
    pc = jnp.stack([pc, along_y(pc)])
    pa = jnp.stack([pa] + [along_z(pa, s) for s in (1, 2, 3)], axis=1)
    pb = jnp.stack([pb, along_y(pb)], axis=1)
    pc = jnp.stack([pc, along_x(pc)])
    pieces = jnp.concatenate(
        [pa.reshape(2, 8 * ra, lanes), pb.reshape(2, 8 * rb, lanes), pc.reshape(2, 8 * rc, lanes)],
        axis=1,
    )

    order = []
    for r, (off, count, axes) in enumerate(((0, ra, "sy"), (ra, rb, "ys"), (ra + rb, rc, "ys"))):
        grid = np.indices((4, 2, count) if axes == "sy" else (2, 4, count)).reshape(3, -1)
        s, yr = (grid[0], grid[1]) if axes == "sy" else (grid[1], grid[0])
        order.append(np.stack([s, yr, off + grid[2]]))
    order = np.concatenate(order, axis=1).astype(np.int32)
    block = ((z - order[0]) % 4) * 4 + (y ^ order[1]) * 2
    per = weight.shape[2]
    everything = jnp.arange(channels, dtype=jnp.int32)
    pick_own = ((block + core) * per + order[2])[:, None] == everything[None, :]
    pick_other = ((block + 1 - core) * per + order[2])[:, None] == everything[None, :]
    pick = jnp.concatenate([pick_own, pick_other]).astype(BF)
    rows = order.shape[1]

    banded = with_halo(latents)
    x = wide_cells(jnp.concatenate([banded, along_core(banded)]))
    t = mm(pick, target.reshape(cells, channels), NT).astype(BF)
    t = jnp.concatenate([t[:rows], along_core(t[rows:])], axis=1)

    kernel, student, error, a0, a1, a2, a3, b0, b1, c0, c1 = vmem_call(
        functools.partial(routed_kernel, width),
        (shape(rows, TAPS * channels), shape(rows, 2 * cells), shape(rows, 2 * cells))
        + (shape(2, 2 * ra, lanes),) * 4
        + (shape(2, 4 * rb, lanes),) * 2
        + (shape(8 * rc, lanes),) * 2,
        1,
        half.astype(jnp.int32).reshape(1),
        pieces,
        x,
        t,
        scratch=[pltpu.VMEM((TAPS, rows, 128), F32)],
    )

    def plus(*terms):
        total = terms[0].astype(F32)
        for term in terms[1:]:
            total = total + term.astype(F32)
        return total

    gb = along_y(b1)
    gc = along_x(c1)
    az = [along_z(v, -s) for s, v in ((1, a1), (2, a2), (3, a3))]
    gb_out = plus(b0[1], gb[1]).astype(BF)
    gc = gc.reshape(2, 4 * rc, lanes)
    c0 = c0.reshape(2, 4 * rc, lanes)
    gc_out = plus(c0[1], gc[1]).astype(BF)
    gb2 = along_x(gb_out)
    gc2 = along_y(gc_out)
    gb = plus(b0[0], gb[0], gb2).astype(BF).reshape(4, rb, lanes)
    gc = plus(c0[0], gc[0], gc2).astype(BF).reshape(4, rc, lanes)
    gbc = jnp.concatenate([gb, gc], axis=1)
    bcz = [along_z(gbc[s], -s) for s in (1, 2, 3)]
    ga = plus(a0, *az).reshape(2, 2, ra, lanes)
    ga_in = along_y(ga[:, 1].astype(BF))
    ga = plus(ga[:, 0], ga_in)
    ga_in = along_x(ga[1].astype(BF))
    ga = plus(ga[0], ga_in)
    grad = jnp.concatenate([ga, plus(gbc[0], *bcz)], axis=0) / F32(b * lax.axis_size("dp"))
    grad = jnp.concatenate(
        [
            grad[:, : TAPS * 256].reshape(-1, TAPS, 256),
            grad[:, TAPS * 256 : TAPS * 320].reshape(-1, TAPS, 64),
        ],
        axis=2,
    )
    grad = jnp.where(half == 0, grad, jnp.roll(grad, 64, axis=2)).transpose(1, 2, 0)

    both = jnp.concatenate([student[:, :cells], along_core(student[:, cells:])])
    out = mm(both, pick, (((0,), (0,)), ((), ()))).astype(BF).reshape(latents.shape)

    error = error.T.reshape(2, band, width, rows)
    back = vmem_call(
        functools.partial(back_kernel, width),
        shape(2, cells, channels, dtype=F32),
        0,
        kernel,
        back_cells(with_halo(error)),
    )
    input_grad = (back[0] + along_core(back[1])).astype(BF).reshape(latents.shape)
    return (out, input_grad, *adam(weight, moment1, moment2, grad))


def solution(mesh):
    def per_device(latents, target, weight, moment1, moment2):
        routed = (
            mesh.shape["dp"] == 16
            and mesh.shape["rows"] == 2
            and latents.shape[0] == 1
            and weight.shape == (TAPS, 320, 40)
        )
        return (routed_device if routed else general_device)(
            latents, target, weight, moment1, moment2
        )

    cells = P("dp", "rows", None, None)
    weights = P(None, "rows", "dp")
    return jax.shard_map(
        per_device,
        mesh=mesh,
        in_specs=(cells, cells, weights, weights, weights),
        out_specs=(cells, cells, weights, weights, weights),
        check_vma=False,
    )
```

```python
import functools

import jax
import jax.numpy as jnp
import numpy as np
from jax import lax
from jax.experimental import pallas as pl
from jax.experimental.pallas import tpu as pltpu
from jax.sharding import PartitionSpec as P

BF = jnp.bfloat16
F32 = jnp.float32
NT = (((1,), (1,)), ((), ()))
NN = (((1,), (0,)), ((), ()))
VMEM_LIMIT = 48 << 20
TAPS = 9
ROUTES = (8, 32)


def mm(a, b, dims):
    return lax.dot_general(a, b, dims, preferred_element_type=F32)


def conv_student(kernel_ref, x_ref, t_ref, s_ref, e_ref, width):
    wide = x_ref.shape[2]
    cells = x_ref.shape[1] - 2 * width
    for l in range(x_ref.shape[0]):
        at = slice(l * cells, (l + 1) * cells)
        total = None
        for a in range(3):
            term = mm(
                kernel_ref[:, a * wide : (a + 1) * wide],
                x_ref[l, a * width : a * width + cells, :],
                NT,
            )
            total = term if total is None else total + term
        student = total.astype(BF)
        s_ref[:, at] = student
        e_ref[:, at] = (student.astype(F32) - t_ref[:, at].astype(F32)).astype(BF)


def tap_grad(x_ref, e_ref, tap, width):
    a, c = divmod(tap, 3)
    channels = x_ref.shape[2] // 3
    cells = x_ref.shape[1] - 2 * width
    total = None
    for l in range(x_ref.shape[0]):
        term = mm(
            e_ref[:, l * cells : (l + 1) * cells],
            x_ref[l, a * width : a * width + cells, c * channels : (c + 1) * channels],
            NN,
        )
        total = term if total is None else total + term
    return total


def plain_kernel(width, kernel_ref, x_ref, t_ref, s_ref, e_ref, g_ref):
    channels = x_ref.shape[2] // 3
    conv_student(kernel_ref, x_ref, t_ref, s_ref, e_ref, width)
    for tap in range(TAPS):
        g_ref[:, tap * channels : (tap + 1) * channels] = tap_grad(
            x_ref, e_ref, tap, width
        ).astype(BF)


def routed_kernel(
    width, place_ref, a0, a1, a2, a3, own_ref, near_ref, far_ref, x_ref, t_ref, k_ref, s_ref, e_ref, *outs
):
    g_refs, (keep_ref, send_ref, mid_ref) = outs[:4], outs[4:]
    a_refs = (a0, a1, a2, a3)
    first, on_core0 = place_ref[0] == 0, place_ref[1] == 0
    rows = k_ref.shape[0]
    low = lax.broadcasted_iota(jnp.int32, (rows, 128), 1) < 64
    spare = TAPS * 256

    def load(at):
        near, far = near_ref[:, at], far_ref[0, :, at]
        own = [r[0, :, at] for r in a_refs] + [own_ref[:, at], jnp.where(on_core0, far, near)]
        other = [r[1, :, at] for r in a_refs] + [jnp.where(on_core0, near, far), far_ref[1, :, at]]
        own, other = jnp.concatenate(own), jnp.concatenate(other)
        return jnp.where(first, own, other), jnp.where(first, other, own)

    for tap in range(TAPS):
        left, right = load(slice(tap * 256, (tap + 1) * 256))
        k_ref[:, tap * 640 : tap * 640 + 256] = left
        k_ref[:, tap * 640 + 384 : (tap + 1) * 640] = right
    for pair in range(5):
        left, right = load(slice(spare + pair * 128, spare + (pair + 1) * 128))
        left, right = left.astype(F32), right.astype(F32)
        k_ref[:, 2 * pair * 640 + 256 : 2 * pair * 640 + 384] = jnp.where(
            low, left, pltpu.roll(right, 64, 1)
        ).astype(BF)
        if 2 * pair + 1 < TAPS:
            k_ref[:, (2 * pair + 1) * 640 + 256 : (2 * pair + 1) * 640 + 384] = jnp.where(
                low, pltpu.roll(left, 64, 1), right
            ).astype(BF)
    conv_student(k_ref, x_ref, t_ref, s_ref, e_ref, width)

    def put(at, left, right):
        left, right = left.astype(BF), right.astype(BF)
        own, other = jnp.where(first, left, right), jnp.where(first, right, left)
        for s in range(4):
            g_refs[s][0, :, at] = own[s * 16 : (s + 1) * 16]
            g_refs[s][1, :, at] = other[s * 16 : (s + 1) * 16]
        own_far, other_near = own[192:], other[64:192]
        keep_ref[0, :, at] = own[64:192]
        send_ref[1, :, at] = other[192:]
        send_ref[0, :, at] = jnp.where(on_core0, own_far, other_near)
        keep_ref[1, :, at] = jnp.where(on_core0, other_near, own_far)

    for tap in range(TAPS):
        grad = tap_grad(x_ref, e_ref, tap, width)
        put(slice(tap * 256, (tap + 1) * 256), grad[:, :256], grad[:, 384:])
        mid_ref[tap] = grad[:, 256:384]
    for pair in range(5):
        even = mid_ref[2 * pair]
        odd = mid_ref[2 * pair + 1] if 2 * pair + 1 < TAPS else jnp.zeros_like(even)
        put(
            slice(spare + pair * 128, spare + (pair + 1) * 128),
            jnp.where(low, even, pltpu.roll(odd, 64, 1)),
            jnp.where(low, pltpu.roll(even, 64, 1), odd),
        )


def back_kernel(width, kernel_ref, e_ref, *out_refs):
    channels = kernel_ref.shape[1] // TAPS
    cells = e_ref.shape[2] - 2 * width
    for l in range(e_ref.shape[1]):
        total = None
        for tap in range(TAPS):
            a, c = divmod(tap, 3)
            term = mm(
                e_ref[c, l, (2 - a) * width : (2 - a) * width + cells, :],
                kernel_ref[:, tap * channels : (tap + 1) * channels],
                NN,
            )
            total = term if total is None else total + term
        out_refs[l][...] = total


def vmem_call(kernel, outs, scalars, *args, scratch=()):
    flops = 2 * 1024 * 320 * 5760
    return pl.pallas_call(
        kernel,
        out_shape=outs,
        in_specs=[pl.BlockSpec(memory_space=pltpu.SMEM)] * scalars
        + [pl.BlockSpec(memory_space=pltpu.VMEM)] * (len(args) - scalars),
        out_specs=jax.tree.map(lambda _: pl.BlockSpec(memory_space=pltpu.VMEM), outs),
        scratch_shapes=scratch,
        cost_estimate=pl.CostEstimate(flops=flops, bytes_accessed=8 << 20, transcendentals=0),
        compiler_params=pltpu.CompilerParams(vmem_limit_bytes=VMEM_LIMIT),
    )(*args)


def shape(*dims, dtype=BF):
    return jax.ShapeDtypeStruct(dims, dtype)


def column_shift(cells, by):
    if by == 0:
        return cells
    zero = jnp.zeros_like(cells[:, :, :1])
    if by > 0:
        return jnp.concatenate([cells[:, :, 1:], zero], axis=2)
    return jnp.concatenate([zero, cells[:, :, :-1]], axis=2)


def adam(weight, moment1, moment2, grad):
    new_moment1 = 0.9 * moment1 + 0.1 * grad
    new_moment2 = 0.999 * moment2 + 0.001 * grad * grad
    new_weight = weight - 0.01 * new_moment1 / (jnp.sqrt(new_moment2) + 1e-08)
    return new_weight, new_moment1, new_moment2


def with_halo(cells):
    count = lax.axis_size("rows")
    if count == 2:
        at_top = lax.axis_index("rows") == 0
        edge = jnp.where(at_top, cells[:, -1:], cells[:, :1])
        got = lax.ppermute(edge, "rows", [(0, 1), (1, 0)])
        zero = jnp.zeros_like(got)
        return jnp.concatenate(
            [jnp.where(at_top, zero, got), cells, jnp.where(at_top, got, zero)], axis=1
        )
    up = lax.ppermute(cells[:, -1:], "rows", [(i, i + 1) for i in range(count - 1)])
    down = lax.ppermute(cells[:, :1], "rows", [(i + 1, i) for i in range(count - 1)])
    return jnp.concatenate([up, cells, down], axis=1)


def wide_cells(cells):
    b, h, w, c = cells.shape
    return jnp.concatenate([column_shift(cells, k - 1) for k in range(3)], axis=3).reshape(
        b, h * w, 3 * c
    )


def back_cells(error):
    b, h, w, n = error.shape
    return jnp.stack([column_shift(error, 1 - k) for k in range(3)]).reshape(3, b, h * w, n)


def general_device(latents, target, weight, moment1, moment2):
    b, band, width, channels = latents.shape
    cells = b * band * width
    part, outs = weight.shape[1], weight.shape[2]
    row_count = lax.axis_size("rows")
    packed = weight.astype(BF).transpose(2, 0, 1)
    gathered = lax.all_gather(packed, "dp", axis=0, tiled=True)
    kernel = lax.all_gather(gathered, "rows", axis=2, tiled=True)
    total_out = kernel.shape[0]
    kernel = kernel.reshape(total_out, TAPS * channels)
    x = wide_cells(with_halo(latents))
    t = target.reshape(cells, total_out).T
    student, error, grad = vmem_call(
        functools.partial(plain_kernel, width),
        (shape(total_out, cells), shape(total_out, cells), shape(total_out, TAPS * channels)),
        0,
        kernel,
        x,
        t,
    )
    error = error.T.reshape(b, band, width, total_out)
    back = vmem_call(
        functools.partial(back_kernel, width),
        (shape(band * width, channels, dtype=F32),) * b,
        0,
        kernel,
        back_cells(with_halo(error)),
    )
    grad = grad.astype(F32).reshape(total_out, TAPS, row_count, part).transpose(2, 0, 1, 3)
    grad = lax.psum_scatter(grad, "rows", scatter_dimension=0, tiled=True)[0]
    grad = lax.psum_scatter(grad, "dp", scatter_dimension=0, tiled=True)
    grad = grad.transpose(1, 2, 0) / F32(b * lax.axis_size("dp"))
    return (
        student.T.reshape(latents.shape),
        jnp.stack(back).astype(BF).reshape(latents.shape),
        *adam(weight, moment1, moment2, grad),
    )


def hop(pairs_of):
    pairs = []
    for i in range(32):
        z, y, core, x = i // 8, i // 4 % 2, i // 2 % 2, i % 2
        z, y, core, x = pairs_of(z, y, core, x)
        pairs.append((i, ((z % 4 * 2 + y) * 2 + core) * 2 + x))
    return lambda v: lax.ppermute(v, ("dp", "rows"), pairs)


def routed_device(latents, target, weight, moment1, moment2):
    b, band, width, channels = latents.shape
    cells = band * width
    index = lax.axis_index("dp")
    core, y, z = index % 2, (index // 2) % 2, index // 4
    half = lax.axis_index("rows")
    along_core = hop(lambda z, y, core, x: (z, y, 1 - core, x))
    along_xy = hop(lambda z, y, core, x: (z, y ^ core, core, x ^ 1 ^ core))
    along_yx = hop(lambda z, y, core, x: (z, y ^ 1 ^ core, core, x ^ core))
    along_z = lambda v, s: hop(lambda z, y, core, x: (z + s, y, core, x))(v)
    ra, rb = ROUTES
    lanes = TAPS * 256 + 640

    piece = weight.transpose(2, 0, 1)
    piece = jnp.where(half == 0, piece, jnp.roll(piece, -64, axis=2)).astype(BF)
    piece = jnp.concatenate(
        [
            piece[:, :, :256].reshape(-1, TAPS * 256),
            piece[:, :, 256:].reshape(-1, TAPS * 64),
            jnp.zeros((piece.shape[0], 64), BF),
        ],
        axis=1,
    )

    def turned(v):
        return jnp.where(core == 0, v.swapaxes(0, 1), v)

    pa, pb = piece[:ra], piece[ra:]
    own = jnp.concatenate([pb] + [along_z(pb, s) for s in (1, 2, 3)])
    pa = jnp.stack([pa, along_xy(pa)])
    pa = turned(jnp.stack([pa, along_yx(pa)])).reshape(2, 2 * ra, lanes)
    near = along_xy(own)
    az = [pa] + [along_z(pa, s) for s in (1, 2, 3)]
    far = along_yx(jnp.stack([own, near]))

    at_a = np.indices((4, 2, ra)).reshape(3, -1)
    at_b = np.indices((2, 4, rb)).reshape(3, -1)
    dist_z = np.concatenate([at_a[0], at_b[1]]).astype(np.int32)
    dist_y = np.concatenate([at_a[1], at_b[0]]).astype(np.int32)
    within = np.concatenate([at_a[2], ra + at_b[2]]).astype(np.int32)
    block = ((z - dist_z) % 4) * 4 + (y ^ dist_y) * 2
    per = weight.shape[2]
    everything = jnp.arange(channels, dtype=jnp.int32)
    pick_own = ((block + core) * per + within)[:, None] == everything[None, :]
    pick_other = ((block + 1 - core) * per + within)[:, None] == everything[None, :]
    pick = jnp.concatenate([pick_own, pick_other]).astype(BF)
    rows = within.shape[0]

    banded = with_halo(latents)
    x = wide_cells(jnp.concatenate([banded, along_core(banded)]))
    t = mm(pick, target.reshape(cells, channels), NT).astype(BF)
    t = jnp.concatenate([t[:rows], along_core(t[rows:])], axis=1)

    kernel, student, error, g0, g1, g2, g3, keep, send = vmem_call(
        functools.partial(routed_kernel, width),
        (shape(rows, TAPS * channels), shape(rows, 2 * cells), shape(rows, 2 * cells))
        + (shape(2, 2 * ra, lanes),) * 4
        + (shape(2, 4 * rb, lanes),) * 2,
        1,
        jnp.stack([half, core]).astype(jnp.int32),
        *az,
        own,
        near,
        far,
        x,
        t,
        scratch=[pltpu.VMEM((TAPS, rows, 128), F32)],
    )

    def plus(*terms):
        total = terms[0].astype(F32)
        for term in terms[1:]:
            total = total + term.astype(F32)
        return total

    got = along_yx(send)
    az = [along_z(v, -s) for s, v in ((1, g1), (2, g2), (3, g3))]
    got2 = along_xy(plus(keep[1], got[1]).astype(BF))
    gb = plus(keep[0], got[0], got2).astype(BF).reshape(4, rb, lanes)
    bz = [along_z(gb[s], -s) for s in (1, 2, 3)]
    ga = turned(plus(g0, *az).reshape(2, 2, ra, lanes))
    ga_in = along_yx(ga[1].astype(BF))
    ga = plus(ga[0], ga_in)
    ga = plus(ga[0], along_xy(ga[1].astype(BF)))
    grad = jnp.concatenate([ga, plus(gb[0], *bz)], axis=0) / F32(b * lax.axis_size("dp"))
    grad = jnp.concatenate(
        [
            grad[:, : TAPS * 256].reshape(-1, TAPS, 256),
            grad[:, TAPS * 256 : TAPS * 320].reshape(-1, TAPS, 64),
        ],
        axis=2,
    )
    grad = jnp.where(half == 0, grad, jnp.roll(grad, 64, axis=2)).transpose(1, 2, 0)

    both = jnp.concatenate([student[:, :cells], along_core(student[:, cells:])])
    out = mm(both, pick, (((0,), (0,)), ((), ()))).astype(BF).reshape(latents.shape)

    error = error.T.reshape(2, band, width, rows)
    back_own, back_other = vmem_call(
        functools.partial(back_kernel, width),
        (shape(cells, channels, dtype=F32),) * 2,
        0,
        kernel,
        back_cells(with_halo(error)),
    )
    input_grad = (back_own + along_core(back_other)).astype(BF).reshape(latents.shape)
    return (out, input_grad, *adam(weight, moment1, moment2, grad))


def solution(mesh):
    def per_device(latents, target, weight, moment1, moment2):
        routed = (
            mesh.shape["dp"] == 16
            and mesh.shape["rows"] == 2
            and latents.shape[0] == 1
            and weight.shape == (TAPS, 320, 40)
        )
        return (routed_device if routed else general_device)(
            latents, target, weight, moment1, moment2
        )

    cells = P("dp", "rows", None, None)
    weights = P(None, "rows", "dp")
    return jax.shard_map(
        per_device,
        mesh=mesh,
        in_specs=(cells, cells, weights, weights, weights),
        out_specs=(cells, cells, weights, weights, weights),
        check_vma=False,
    )
```

```python
import functools

import jax
import jax.numpy as jnp
import numpy as np
from jax import lax
from jax.experimental import pallas as pl
from jax.experimental.pallas import tpu as pltpu
from jax.sharding import PartitionSpec as P

BF = jnp.bfloat16
F32 = jnp.float32
NT = (((1,), (1,)), ((), ()))
NN = (((1,), (0,)), ((), ()))
VMEM_LIMIT = 28 << 20
TAPS = 9
CHUNKS = (24, 16)


def mm(a, b, dims):
    return lax.dot_general(a, b, dims, preferred_element_type=F32)


def conv_student(kernel_ref, x_ref, t_ref, s_ref, e_ref, width, by_cell=None):
    wide = x_ref.shape[2]
    cells = x_ref.shape[1] - 2 * width
    for l in range(x_ref.shape[0]):
        at = slice(l * cells, (l + 1) * cells)
        total = None
        for a in range(3):
            term = mm(
                kernel_ref[:, a * wide : (a + 1) * wide],
                x_ref[l, a * width : a * width + cells, :],
                NT,
            )
            total = term if total is None else total + term
        student = total.astype(BF)
        s_ref[:, at] = student
        error = student.astype(F32) - t_ref[:, at].astype(F32)
        e_ref[:, at] = error.astype(BF)
        if by_cell is not None:
            by_cell[at, :] = error.T.astype(BF)


def tap_grad(x_ref, e_ref, tap, width):
    a, c = divmod(tap, 3)
    channels = x_ref.shape[2] // 3
    cells = x_ref.shape[1] - 2 * width
    total = None
    for l in range(x_ref.shape[0]):
        term = mm(
            e_ref[:, l * cells : (l + 1) * cells],
            x_ref[l, a * width : a * width + cells, c * channels : (c + 1) * channels],
            NN,
        )
        total = term if total is None else total + term
    return total


def plain_kernel(width, kernel_ref, x_ref, t_ref, s_ref, e_ref, g_ref):
    channels = x_ref.shape[2] // 3
    conv_student(kernel_ref, x_ref, t_ref, s_ref, e_ref, width)
    for tap in range(TAPS):
        g_ref[:, tap * channels : (tap + 1) * channels] = tap_grad(
            x_ref, e_ref, tap, width
        ).astype(BF)


def routed_kernel(
    width, place_ref, own_ref, near_ref, far_ref, x_ref, t_ref, k_ref, s_ref, e_ref, keep_ref, send_ref, mid_ref, flat_ref
):
    first, on_core0 = place_ref[0] == 0, place_ref[1] == 0
    rows = k_ref.shape[0]
    near_y, far_y = slice(0, rows // 2), slice(rows // 2, rows)
    low = lax.broadcasted_iota(jnp.int32, (rows, 128), 1) < 64
    spare = TAPS * 256

    def load(at):
        near, far = near_ref[:, at], far_ref[0, :, at]
        own = jnp.concatenate([own_ref[:, at], jnp.where(on_core0, far, near)])
        other = jnp.concatenate([jnp.where(on_core0, near, far), far_ref[1, :, at]])
        return jnp.where(first, own, other), jnp.where(first, other, own)

    for tap in range(TAPS):
        left, right = load(slice(tap * 256, (tap + 1) * 256))
        k_ref[:, tap * 640 : tap * 640 + 256] = left
        k_ref[:, tap * 640 + 384 : (tap + 1) * 640] = right
    for pair in range(5):
        left, right = load(slice(spare + pair * 128, spare + (pair + 1) * 128))
        left, right = left.astype(F32), right.astype(F32)
        k_ref[:, 2 * pair * 640 + 256 : 2 * pair * 640 + 384] = jnp.where(
            low, left, pltpu.roll(right, 64, 1)
        ).astype(BF)
        if 2 * pair + 1 < TAPS:
            k_ref[:, (2 * pair + 1) * 640 + 256 : (2 * pair + 1) * 640 + 384] = jnp.where(
                low, pltpu.roll(left, 64, 1), right
            ).astype(BF)
    conv_student(k_ref, x_ref, t_ref, s_ref, flat_ref, width, e_ref)

    def put(at, left, right):
        left, right = left.astype(BF), right.astype(BF)
        own, other = jnp.where(first, left, right), jnp.where(first, right, left)
        own_far, other_near = own[far_y], other[near_y]
        keep_ref[0, :, at] = own[near_y]
        send_ref[1, :, at] = other[far_y]
        send_ref[0, :, at] = jnp.where(on_core0, own_far, other_near)
        keep_ref[1, :, at] = jnp.where(on_core0, other_near, own_far)

    for tap in range(TAPS):
        grad = tap_grad(x_ref, flat_ref, tap, width)
        put(slice(tap * 256, (tap + 1) * 256), grad[:, :256], grad[:, 384:])
        mid_ref[tap] = grad[:, 256:384]
    for pair in range(5):
        even = mid_ref[2 * pair]
        odd = mid_ref[2 * pair + 1] if 2 * pair + 1 < TAPS else jnp.zeros_like(even)
        put(
            slice(spare + pair * 128, spare + (pair + 1) * 128),
            jnp.where(low, even, pltpu.roll(odd, 64, 1)),
            jnp.where(low, pltpu.roll(even, 64, 1), odd),
        )


def twice(half_tile):
    return jnp.concatenate([half_tile, half_tile], axis=1)


def pack_kernel(place_ref, w_ref, out_ref):
    first = place_ref[0] == 0
    low = lax.broadcasted_iota(jnp.int32, (w_ref.shape[1], 128), 1) < 64
    swap = lambda v: pltpu.roll(v, 64, 1)
    spare = []
    for tap in range(TAPS):
        t0, t1 = w_ref[tap, :, :128], w_ref[tap, :, 128:256]
        t2 = twice(w_ref[tap, :, 256:])
        r1 = swap(t1)
        out_ref[:, tap * 256 : tap * 256 + 128] = jnp.where(
            first, t0, jnp.where(low, swap(t0), r1)
        ).astype(BF)
        out_ref[:, tap * 256 + 128 : (tap + 1) * 256] = jnp.where(
            first, t1, jnp.where(low, r1, t2)
        ).astype(BF)
        spare.append(jnp.where(first, t2, jnp.where(low, t0, swap(t0))))
    spare.append(jnp.zeros_like(spare[0]))
    for pair in range(5):
        at = TAPS * 256 + pair * 128
        out_ref[:, at : at + 128] = jnp.where(low, spare[2 * pair], spare[2 * pair + 1]).astype(BF)


def adam_kernel(scale, place_ref, w_ref, m1_ref, m2_ref, *refs):
    parts, outs = refs[:-3], refs[-3:]
    first = place_ref[0] == 0
    low = lax.broadcasted_iota(jnp.int32, (w_ref.shape[1], 128), 1) < 64
    swap = lambda v: pltpu.roll(v, 64, 1)

    def grad(at):
        sums = []
        for i in range(0, len(parts), 4):
            p0, p1, p2, p3 = [ref[:, at].astype(F32) for ref in parts[i : i + 4]]
            sums.append((p0 + p1) + (p2 + p3))
        return jnp.concatenate(sums) * scale

    for tap in range(TAPS):
        if tap % 2 == 0:
            spare = grad(slice(TAPS * 256 + tap * 64, TAPS * 256 + tap * 64 + 128))
            spare_swap = swap(spare)
        at_low = spare if tap % 2 == 0 else spare_swap
        left = grad(slice(tap * 256, tap * 256 + 128))
        right = grad(slice(tap * 256 + 128, (tap + 1) * 256))
        left_swap, right_swap = swap(left), swap(right)
        tiles = (
            jnp.where(first, left, jnp.where(low, at_low, left_swap)),
            jnp.where(first, right, jnp.where(low, left_swap, right_swap)),
            jnp.where(first, at_low, right_swap)[:, :64],
        )
        for tile, at in zip(tiles, (slice(0, 128), slice(128, 256), slice(256, 320))):
            new = adam(w_ref[tap, :, at], m1_ref[tap, :, at], m2_ref[tap, :, at], tile)
            for out_ref, value in zip(outs, new):
                out_ref[tap, :, at] = value


def back_kernel(width, parts, *refs):
    kernel_refs, e_refs, out_ref = refs[:parts], refs[parts : 2 * parts], refs[-1]
    channels = kernel_refs[0].shape[1] // TAPS
    cells = e_refs[0].shape[1] - 2 * width
    total = None
    for tap in range(TAPS):
        a, c = divmod(tap, 3)
        for kernel_ref, e_ref in zip(kernel_refs, e_refs):
            term = mm(
                e_ref[c, (2 - a) * width : (2 - a) * width + cells, :],
                kernel_ref[:, tap * channels : (tap + 1) * channels],
                NN,
            )
            total = term if total is None else total + term
    out_ref[...] = total


def vmem_call(kernel, outs, scalars, *args, scratch=(), flops=0):
    return pl.pallas_call(
        kernel,
        out_shape=outs,
        in_specs=[pl.BlockSpec(memory_space=pltpu.SMEM)] * scalars
        + [pl.BlockSpec(memory_space=pltpu.VMEM)] * (len(args) - scalars),
        out_specs=jax.tree.map(lambda _: pl.BlockSpec(memory_space=pltpu.VMEM), outs),
        scratch_shapes=scratch,
        cost_estimate=pl.CostEstimate(flops=flops, bytes_accessed=1 << 20, transcendentals=0),
        compiler_params=pltpu.CompilerParams(vmem_limit_bytes=VMEM_LIMIT),
    )(*args)


def shape(*dims, dtype=BF):
    return jax.ShapeDtypeStruct(dims, dtype)


def column_shift(cells, by):
    if by == 0:
        return cells
    zero = jnp.zeros_like(cells[:, :, :1])
    if by > 0:
        return jnp.concatenate([cells[:, :, 1:], zero], axis=2)
    return jnp.concatenate([zero, cells[:, :, :-1]], axis=2)


def adam(weight, moment1, moment2, grad):
    new_moment1 = 0.9 * moment1 + 0.1 * grad
    new_moment2 = 0.999 * moment2 + 0.001 * grad * grad
    new_weight = weight - 0.01 * new_moment1 / (jnp.sqrt(new_moment2) + 1e-08)
    return new_weight, new_moment1, new_moment2


def with_halo(cells):
    count = lax.axis_size("rows")
    if count == 2:
        at_top = lax.axis_index("rows") == 0
        edge = jnp.where(at_top, cells[:, -1:], cells[:, :1])
        got = lax.ppermute(edge, "rows", [(0, 1), (1, 0)])
        zero = jnp.zeros_like(got)
        return jnp.concatenate(
            [jnp.where(at_top, zero, got), cells, jnp.where(at_top, got, zero)], axis=1
        )
    up = lax.ppermute(cells[:, -1:], "rows", [(i, i + 1) for i in range(count - 1)])
    down = lax.ppermute(cells[:, :1], "rows", [(i + 1, i) for i in range(count - 1)])
    return jnp.concatenate([up, cells, down], axis=1)


def wide_cells(cells):
    b, h, w, c = cells.shape
    return jnp.concatenate([column_shift(cells, k - 1) for k in range(3)], axis=3).reshape(
        b, h * w, 3 * c
    )


def back_cells(error):
    b, h, w, n = error.shape
    return jnp.stack([column_shift(error, 1 - k) for k in range(3)]).reshape(3, b, h * w, n)


def general_device(latents, target, weight, moment1, moment2):
    b, band, width, channels = latents.shape
    cells = b * band * width
    part, outs = weight.shape[1], weight.shape[2]
    row_count = lax.axis_size("rows")
    packed = weight.astype(BF).transpose(2, 0, 1)
    gathered = lax.all_gather(packed, "dp", axis=0, tiled=True)
    kernel = lax.all_gather(gathered, "rows", axis=2, tiled=True)
    total_out = kernel.shape[0]
    kernel = kernel.reshape(total_out, TAPS * channels)
    x = wide_cells(with_halo(latents))
    t = target.reshape(cells, total_out).T
    student, error, grad = vmem_call(
        functools.partial(plain_kernel, width),
        (shape(total_out, cells), shape(total_out, cells), shape(total_out, TAPS * channels)),
        0,
        kernel,
        x,
        t,
    )
    error = error.T.reshape(b, band, width, total_out)
    shifted = back_cells(with_halo(error))
    back = [
        vmem_call(
            functools.partial(back_kernel, width, 1),
            shape(band * width, channels, dtype=F32),
            0,
            kernel,
            shifted[:, l],
        )
        for l in range(b)
    ]
    grad = grad.astype(F32).reshape(total_out, TAPS, row_count, part).transpose(2, 0, 1, 3)
    grad = lax.psum_scatter(grad, "rows", scatter_dimension=0, tiled=True)[0]
    grad = lax.psum_scatter(grad, "dp", scatter_dimension=0, tiled=True)
    grad = grad.transpose(1, 2, 0) / F32(b * lax.axis_size("dp"))
    return (
        student.T.reshape(latents.shape),
        jnp.stack(back).astype(BF).reshape(latents.shape),
        *adam(weight, moment1, moment2, grad),
    )


def hop(pairs_of):
    pairs = []
    for i in range(32):
        z, y, core, x = i // 8, i // 4 % 2, i // 2 % 2, i % 2
        z, y, core, x = pairs_of(z, y, core, x)
        pairs.append((i, ((z % 4 * 2 + y) * 2 + core) * 2 + x))
    return lambda v: lax.ppermute(v, ("dp", "rows"), pairs)


def phase(*values):
    return lax.optimization_barrier(values)


def routed_device(latents, target, weight, moment1, moment2):
    b, band, width, channels = latents.shape
    cells = band * width
    index = lax.axis_index("dp")
    core, y, z = index % 2, (index // 2) % 2, index // 4
    half = lax.axis_index("rows")
    along_core = hop(lambda z, y, core, x: (z, y, 1 - core, x))
    along_xy = hop(lambda z, y, core, x: (z, y ^ core, core, x ^ 1 ^ core))
    along_yx = hop(lambda z, y, core, x: (z, y ^ 1 ^ core, core, x ^ core))
    along_z = lambda v, s: hop(lambda z, y, core, x: (z + s, y, core, x))(v)
    lanes = TAPS * 256 + 640

    place = jnp.stack([half, core]).astype(jnp.int32)
    by_tap = lambda v: v.transpose(0, 2, 1)
    per = weight.shape[2]
    piece = vmem_call(pack_kernel, shape(per, lanes), 1, place, by_tap(weight))
    piece, latents, target = phase(piece, latents, target)

    chunk_a, chunk_b = CHUNKS
    grids = [
        np.indices((2, 4, chunk_a)).reshape(3, -1),
        np.indices((2, 4, chunk_b)).reshape(3, -1) + [[0], [0], [chunk_a]],
    ]
    dist_y, dist_z, within = np.concatenate(grids, axis=1).astype(np.int32)
    block = ((z - dist_z) % 4) * 4 + (y ^ dist_y) * 2
    everything = jnp.arange(channels, dtype=jnp.int32)
    pick_own = ((block + core) * per + within)[:, None] == everything[None, :]
    pick_other = ((block + 1 - core) * per + within)[:, None] == everything[None, :]
    pick = jnp.concatenate([pick_own, pick_other]).astype(BF)
    rows = within.shape[0]
    rows_a = 8 * chunk_a

    def plus(*terms):
        total = terms[0].astype(F32)
        for term in terms[1:]:
            total = total + term.astype(F32)
        return total

    bz = [along_z(piece, s) for s in (1, 2, 3)]
    banded = with_halo(latents)
    t = mm(pick, target.reshape(cells, channels), NT).astype(BF)
    bz, banded, t = phase(bz, banded, t)
    t = jnp.concatenate([t[:rows], along_core(t[rows:])], axis=1)
    own_a = jnp.concatenate([v[:chunk_a] for v in [piece] + bz])
    own_b = jnp.concatenate([v[chunk_a:] for v in [piece] + bz])
    near_a, near_b = along_xy(own_a), along_xy(own_b)
    x = wide_cells(jnp.concatenate([banded, along_core(banded)]))
    far_a = along_yx(jnp.stack([own_a, near_a]))
    far_b = along_yx(jnp.stack([own_b, near_b]))

    def compute(own, near, far, t):
        n = t.shape[0]
        return vmem_call(
            functools.partial(routed_kernel, width),
            (shape(n, TAPS * channels), shape(n, 2 * cells), shape(2 * cells, n))
            + (shape(2, n // 2, lanes),) * 2,
            1,
            place,
            own,
            near,
            far,
            x,
            t,
            scratch=[pltpu.VMEM((TAPS, n, 128), F32), pltpu.VMEM((n, 2 * cells), BF)],
            flops=30 * 10**9,
        )

    far_a, near_b, x, t = phase(far_a, near_b, x, t)
    kernel_a, student_a, error_a, keep_a, send_a = compute(own_a, near_a, far_a, t[:rows_a])
    got_a = along_yx(send_a)
    kernel_b, student_b, error_b, keep_b, send_b = compute(own_b, near_b, far_b, t[rows_a:])
    got_b = along_yx(send_b)
    got_a, send_b, error_b = phase(got_a, send_b, error_b)

    got2_a = along_xy(plus(keep_a[1], got_a[1]).astype(BF))
    error = jnp.concatenate([error_a, error_b], axis=1)
    shifted = back_cells(with_halo(error.reshape(2, band, width, rows)))

    def back(l):
        return vmem_call(
            functools.partial(back_kernel, width, 2),
            shape(cells, channels, dtype=F32),
            0,
            kernel_a,
            kernel_b,
            shifted[:, l, :, :rows_a],
            shifted[:, l, :, rows_a:],
            flops=20 * 10**9,
        )

    back_other = back(1)
    got2_a, got_b, back_other, shifted = phase(got2_a, got_b, back_other, shifted)
    back_in = along_core(back_other)
    gb_a = plus(keep_a[0], got_a[0], got2_a).astype(BF).reshape(4, chunk_a, lanes)
    bz_a = [along_z(gb_a[s], -s) for s in (1, 2, 3)]
    got2_b = along_xy(plus(keep_b[1], got_b[1]).astype(BF))
    got2_b, shifted, student_a, student_b = phase(got2_b, shifted, student_a, student_b)
    gb_b = plus(keep_b[0], got_b[0], got2_b).astype(BF).reshape(4, chunk_b, lanes)
    bz_b = [along_z(gb_b[s], -s) for s in (1, 2, 3)]
    back_own = back(0)

    student = jnp.concatenate([student_a, student_b])
    both = jnp.concatenate([student[:, :cells], along_core(student[:, cells:])])
    out = mm(both, pick, (((0,), (0,)), ((), ()))).astype(BF).reshape(latents.shape)
    input_grad = (back_own + back_in).astype(BF).reshape(latents.shape)
    bz_a, bz_b, out, input_grad = phase(bz_a, bz_b, out, input_grad)
    news = vmem_call(
        functools.partial(adam_kernel, 1.0 / (b * lax.axis_size("dp"))),
        (shape(TAPS, per, weight.shape[1], dtype=F32),) * 3,
        1,
        place,
        by_tap(weight),
        by_tap(moment1),
        by_tap(moment2),
        gb_a[0],
        *bz_a,
        gb_b[0],
        *bz_b,
    )
    return (out, input_grad, *map(by_tap, news))


def solution(mesh):
    def per_device(latents, target, weight, moment1, moment2):
        routed = (
            mesh.shape["dp"] == 16
            and mesh.shape["rows"] == 2
            and latents.shape[0] == 1
            and weight.shape == (TAPS, 320, 40)
        )
        return (routed_device if routed else general_device)(
            latents, target, weight, moment1, moment2
        )

    cells = P("dp", "rows", None, None)
    weights = P(None, "rows", "dp")
    return jax.shard_map(
        per_device,
        mesh=mesh,
        in_specs=(cells, cells, weights, weights, weights),
        out_specs=(cells, cells, weights, weights, weights),
        check_vma=False,
    )
```

```python
import functools

import jax
import jax.numpy as jnp
import numpy as np
from jax import lax
from jax.experimental import pallas as pl
from jax.experimental.pallas import tpu as pltpu
from jax.sharding import PartitionSpec as P

BF = jnp.bfloat16
F32 = jnp.float32
NT = (((1,), (1,)), ((), ()))
NN = (((1,), (0,)), ((), ()))
VMEM_LIMIT = 28 << 20
TAPS = 9
CHUNKS = (24, 16)
ROUTE_A = 8


def mm(a, b, dims):
    return lax.dot_general(a, b, dims, preferred_element_type=F32)


def conv_student(kernel_ref, x_ref, t_ref, s_ref, e_ref, width, by_cell=None):
    wide = x_ref.shape[2]
    cells = x_ref.shape[1] - 2 * width
    for l in range(x_ref.shape[0]):
        at = slice(l * cells, (l + 1) * cells)
        total = None
        for a in range(3):
            term = mm(
                kernel_ref[:, a * wide : (a + 1) * wide],
                x_ref[l, a * width : a * width + cells, :],
                NT,
            )
            total = term if total is None else total + term
        student = total.astype(BF)
        s_ref[:, at] = student
        error = student.astype(F32) - t_ref[:, at].astype(F32)
        e_ref[:, at] = error.astype(BF)
        if by_cell is not None:
            by_cell[at, :] = error.T.astype(BF)


def tap_grad(x_ref, e_ref, tap, width):
    a, c = divmod(tap, 3)
    channels = x_ref.shape[2] // 3
    cells = x_ref.shape[1] - 2 * width
    total = None
    for l in range(x_ref.shape[0]):
        term = mm(
            e_ref[:, l * cells : (l + 1) * cells],
            x_ref[l, a * width : a * width + cells, c * channels : (c + 1) * channels],
            NN,
        )
        total = term if total is None else total + term
    return total


def plain_kernel(width, kernel_ref, x_ref, t_ref, s_ref, e_ref, g_ref):
    channels = x_ref.shape[2] // 3
    conv_student(kernel_ref, x_ref, t_ref, s_ref, e_ref, width)
    for tap in range(TAPS):
        g_ref[:, tap * channels : (tap + 1) * channels] = tap_grad(
            x_ref, e_ref, tap, width
        ).astype(BF)


def routed_kernel(width, extra, place_ref, own_ref, near_ref, far_ref, x_ref, t_ref, *refs):
    a_refs, refs = refs[:extra], refs[extra:]
    k_ref, s_ref, e_ref, keep_ref, send_ref, mid_ref, flat_ref = refs
    first, on_core0 = place_ref[0] == 0, place_ref[1] == 0
    rows = k_ref.shape[0]
    near_y, far_y = slice(0, rows // 2), slice(rows // 2, rows)
    low = lax.broadcasted_iota(jnp.int32, (rows, 128), 1) < 64
    spare = TAPS * 256

    def load(at):
        near, far = near_ref[:, at], far_ref[0, :, at]
        own = [own_ref[:, at], jnp.where(on_core0, far, near)]
        other = [jnp.where(on_core0, near, far), far_ref[1, :, at]]
        for a_ref in a_refs:
            half = a_ref.shape[1] // 2
            own = [a_ref[0, :half, at], own[0], a_ref[0, half:, at], own[1]]
            other = [a_ref[1, :half, at], other[0], a_ref[1, half:, at], other[1]]
        own, other = jnp.concatenate(own), jnp.concatenate(other)
        return jnp.where(first, own, other), jnp.where(first, other, own)

    for tap in range(TAPS):
        left, right = load(slice(tap * 256, (tap + 1) * 256))
        k_ref[:, tap * 640 : tap * 640 + 256] = left
        k_ref[:, tap * 640 + 384 : (tap + 1) * 640] = right
    for pair in range(5):
        left, right = load(slice(spare + pair * 128, spare + (pair + 1) * 128))
        left, right = left.astype(F32), right.astype(F32)
        k_ref[:, 2 * pair * 640 + 256 : 2 * pair * 640 + 384] = jnp.where(
            low, left, pltpu.roll(right, 64, 1)
        ).astype(BF)
        if 2 * pair + 1 < TAPS:
            k_ref[:, (2 * pair + 1) * 640 + 256 : (2 * pair + 1) * 640 + 384] = jnp.where(
                low, pltpu.roll(left, 64, 1), right
            ).astype(BF)
    conv_student(k_ref, x_ref, t_ref, s_ref, flat_ref, width, e_ref)

    def put(at, left, right):
        left, right = left.astype(BF), right.astype(BF)
        own, other = jnp.where(first, left, right), jnp.where(first, right, left)
        own_far, other_near = own[far_y], other[near_y]
        keep_ref[0, :, at] = own[near_y]
        send_ref[1, :, at] = other[far_y]
        send_ref[0, :, at] = jnp.where(on_core0, own_far, other_near)
        keep_ref[1, :, at] = jnp.where(on_core0, other_near, own_far)

    for tap in range(TAPS):
        grad = tap_grad(x_ref, flat_ref, tap, width)
        put(slice(tap * 256, (tap + 1) * 256), grad[:, :256], grad[:, 384:])
        mid_ref[tap] = grad[:, 256:384]
    for pair in range(5):
        even = mid_ref[2 * pair]
        odd = mid_ref[2 * pair + 1] if 2 * pair + 1 < TAPS else jnp.zeros_like(even)
        put(
            slice(spare + pair * 128, spare + (pair + 1) * 128),
            jnp.where(low, even, pltpu.roll(odd, 64, 1)),
            jnp.where(low, pltpu.roll(even, 64, 1), odd),
        )


def twice(half_tile):
    return jnp.concatenate([half_tile, half_tile], axis=1)


def pack_kernel(place_ref, w_ref, out_ref):
    first = place_ref[0] == 0
    low = lax.broadcasted_iota(jnp.int32, (w_ref.shape[1], 128), 1) < 64
    swap = lambda v: pltpu.roll(v, 64, 1)
    spare = []
    for tap in range(TAPS):
        t0, t1 = w_ref[tap, :, :128], w_ref[tap, :, 128:256]
        t2 = twice(w_ref[tap, :, 256:])
        r1 = swap(t1)
        out_ref[:, tap * 256 : tap * 256 + 128] = jnp.where(
            first, t0, jnp.where(low, swap(t0), r1)
        ).astype(BF)
        out_ref[:, tap * 256 + 128 : (tap + 1) * 256] = jnp.where(
            first, t1, jnp.where(low, r1, t2)
        ).astype(BF)
        spare.append(jnp.where(first, t2, jnp.where(low, t0, swap(t0))))
    spare.append(jnp.zeros_like(spare[0]))
    for pair in range(5):
        at = TAPS * 256 + pair * 128
        out_ref[:, at : at + 128] = jnp.where(low, spare[2 * pair], spare[2 * pair + 1]).astype(BF)


def adam_kernel(scale, place_ref, w_ref, m1_ref, m2_ref, *refs):
    parts, outs = refs[:-3], refs[-3:]
    first = place_ref[0] == 0
    low = lax.broadcasted_iota(jnp.int32, (w_ref.shape[1], 128), 1) < 64
    swap = lambda v: pltpu.roll(v, 64, 1)

    def grad(at):
        sums = []
        for i in range(0, len(parts), 3):
            p0, p1, p2 = [ref[:, at].astype(F32) for ref in parts[i : i + 3]]
            sums.append((p0 + p1) + p2)
        return jnp.concatenate(sums) * scale

    for tap in range(TAPS):
        if tap % 2 == 0:
            spare = grad(slice(TAPS * 256 + tap * 64, TAPS * 256 + tap * 64 + 128))
            spare_swap = swap(spare)
        at_low = spare if tap % 2 == 0 else spare_swap
        left = grad(slice(tap * 256, tap * 256 + 128))
        right = grad(slice(tap * 256 + 128, (tap + 1) * 256))
        left_swap, right_swap = swap(left), swap(right)
        tiles = (
            jnp.where(first, left, jnp.where(low, at_low, left_swap)),
            jnp.where(first, right, jnp.where(low, left_swap, right_swap)),
            jnp.where(first, at_low, right_swap)[:, :64],
        )
        for tile, at in zip(tiles, (slice(0, 128), slice(128, 256), slice(256, 320))):
            new = adam(w_ref[tap, :, at], m1_ref[tap, :, at], m2_ref[tap, :, at], tile)
            for out_ref, value in zip(outs, new):
                out_ref[tap, :, at] = value


def back_kernel(width, parts, *refs):
    kernel_refs, e_refs, out_ref = refs[:parts], refs[parts : 2 * parts], refs[-1]
    channels = kernel_refs[0].shape[1] // TAPS
    cells = e_refs[0].shape[1] - 2 * width
    total = None
    for tap in range(TAPS):
        a, c = divmod(tap, 3)
        for kernel_ref, e_ref in zip(kernel_refs, e_refs):
            term = mm(
                e_ref[c, (2 - a) * width : (2 - a) * width + cells, :],
                kernel_ref[:, tap * channels : (tap + 1) * channels],
                NN,
            )
            total = term if total is None else total + term
    out_ref[...] = total


def vmem_call(kernel, outs, scalars, *args, scratch=(), flops=0):
    return pl.pallas_call(
        kernel,
        out_shape=outs,
        in_specs=[pl.BlockSpec(memory_space=pltpu.SMEM)] * scalars
        + [pl.BlockSpec(memory_space=pltpu.VMEM)] * (len(args) - scalars),
        out_specs=jax.tree.map(lambda _: pl.BlockSpec(memory_space=pltpu.VMEM), outs),
        scratch_shapes=scratch,
        cost_estimate=pl.CostEstimate(flops=flops, bytes_accessed=1 << 20, transcendentals=0),
        compiler_params=pltpu.CompilerParams(vmem_limit_bytes=VMEM_LIMIT),
    )(*args)


def shape(*dims, dtype=BF):
    return jax.ShapeDtypeStruct(dims, dtype)


def column_shift(cells, by):
    if by == 0:
        return cells
    zero = jnp.zeros_like(cells[:, :, :1])
    if by > 0:
        return jnp.concatenate([cells[:, :, 1:], zero], axis=2)
    return jnp.concatenate([zero, cells[:, :, :-1]], axis=2)


def adam(weight, moment1, moment2, grad):
    new_moment1 = 0.9 * moment1 + 0.1 * grad
    new_moment2 = 0.999 * moment2 + 0.001 * grad * grad
    new_weight = weight - 0.01 * new_moment1 / (jnp.sqrt(new_moment2) + 1e-08)
    return new_weight, new_moment1, new_moment2


def with_halo(cells):
    count = lax.axis_size("rows")
    if count == 2:
        at_top = lax.axis_index("rows") == 0
        edge = jnp.where(at_top, cells[:, -1:], cells[:, :1])
        got = lax.ppermute(edge, "rows", [(0, 1), (1, 0)])
        zero = jnp.zeros_like(got)
        return jnp.concatenate(
            [jnp.where(at_top, zero, got), cells, jnp.where(at_top, got, zero)], axis=1
        )
    up = lax.ppermute(cells[:, -1:], "rows", [(i, i + 1) for i in range(count - 1)])
    down = lax.ppermute(cells[:, :1], "rows", [(i + 1, i) for i in range(count - 1)])
    return jnp.concatenate([up, cells, down], axis=1)


def wide_cells(cells):
    b, h, w, c = cells.shape
    return jnp.concatenate([column_shift(cells, k - 1) for k in range(3)], axis=3).reshape(
        b, h * w, 3 * c
    )


def back_cells(error):
    b, h, w, n = error.shape
    return jnp.stack([column_shift(error, 1 - k) for k in range(3)]).reshape(3, b, h * w, n)


def general_device(latents, target, weight, moment1, moment2):
    b, band, width, channels = latents.shape
    cells = b * band * width
    part, outs = weight.shape[1], weight.shape[2]
    row_count = lax.axis_size("rows")
    packed = weight.astype(BF).transpose(2, 0, 1)
    gathered = lax.all_gather(packed, "dp", axis=0, tiled=True)
    kernel = lax.all_gather(gathered, "rows", axis=2, tiled=True)
    total_out = kernel.shape[0]
    kernel = kernel.reshape(total_out, TAPS * channels)
    x = wide_cells(with_halo(latents))
    t = target.reshape(cells, total_out).T
    student, error, grad = vmem_call(
        functools.partial(plain_kernel, width),
        (shape(total_out, cells), shape(total_out, cells), shape(total_out, TAPS * channels)),
        0,
        kernel,
        x,
        t,
    )
    error = error.T.reshape(b, band, width, total_out)
    shifted = back_cells(with_halo(error))
    back = [
        vmem_call(
            functools.partial(back_kernel, width, 1),
            shape(band * width, channels, dtype=F32),
            0,
            kernel,
            shifted[:, l],
        )
        for l in range(b)
    ]
    grad = grad.astype(F32).reshape(total_out, TAPS, row_count, part).transpose(2, 0, 1, 3)
    grad = lax.psum_scatter(grad, "rows", scatter_dimension=0, tiled=True)[0]
    grad = lax.psum_scatter(grad, "dp", scatter_dimension=0, tiled=True)
    grad = grad.transpose(1, 2, 0) / F32(b * lax.axis_size("dp"))
    return (
        student.T.reshape(latents.shape),
        jnp.stack(back).astype(BF).reshape(latents.shape),
        *adam(weight, moment1, moment2, grad),
    )


def hop(pairs_of):
    pairs = []
    for i in range(32):
        z, y, core, x = i // 8, i // 4 % 2, i // 2 % 2, i % 2
        z, y, core, x = pairs_of(z, y, core, x)
        pairs.append((i, ((z % 4 * 2 + y) * 2 + core) * 2 + x))
    return lambda v: lax.ppermute(v, ("dp", "rows"), pairs)


def phase(*values):
    return lax.optimization_barrier(values)


def routed_device(latents, target, weight, moment1, moment2):
    b, band, width, channels = latents.shape
    cells = band * width
    index = lax.axis_index("dp")
    core, y, z = index % 2, (index // 2) % 2, index // 4
    half = lax.axis_index("rows")
    along_core = hop(lambda z, y, core, x: (z, y, 1 - core, x))
    along_xy = hop(lambda z, y, core, x: (z, y ^ core, core, x ^ 1 ^ core))
    along_yx = hop(lambda z, y, core, x: (z, y ^ 1 ^ core, core, x ^ core))
    along_z = lambda v, s: hop(lambda z, y, core, x: (z + s, y, core, x))(v)
    along_pair = hop(lambda z, y, core, x: (z ^ 1, y, core, x))
    lanes = TAPS * 256 + 640

    place = jnp.stack([half, core]).astype(jnp.int32)
    by_tap = lambda v: v.transpose(0, 2, 1)
    per = weight.shape[2]
    piece = vmem_call(pack_kernel, shape(per, lanes), 1, place, by_tap(weight))
    piece, latents, target = phase(piece, latents, target)

    def turned(v):
        return jnp.where(core == 0, v.swapaxes(0, 1), v)

    chunk_a, chunk_b = CHUNKS
    grids = []
    for begin, counts in ((0, (ROUTE_A, chunk_a - ROUTE_A)), (chunk_a, (chunk_b,))):
        for dist_y in range(2):
            at = begin
            for count in counts:
                dist_z, within = np.indices((4, count)).reshape(2, -1)
                grids.append(np.stack([np.full_like(dist_z, dist_y), dist_z, at + within]))
                at += count
    dist_y, dist_z, within = np.concatenate(grids, axis=1).astype(np.int32)
    block = ((z - dist_z) % 4) * 4 + (y ^ dist_y) * 2
    everything = jnp.arange(channels, dtype=jnp.int32)
    pick_own = ((block + core) * per + within)[:, None] == everything[None, :]
    pick_other = ((block + 1 - core) * per + within)[:, None] == everything[None, :]
    pick = jnp.concatenate([pick_own, pick_other]).astype(BF)
    rows = within.shape[0]
    rows_a = 8 * chunk_a

    def plus(*terms):
        total = terms[0].astype(F32)
        for term in terms[1:]:
            total = total + term.astype(F32)
        return total

    pa, pb = piece[:ROUTE_A], piece[ROUTE_A:]
    bz = [along_z(pb, s) for s in (1, 2, 3)]
    pa = jnp.stack([pa, along_xy(pa)])
    t = mm(pick, target.reshape(cells, channels), NT).astype(BF)
    pa, latents, t = phase(pa, latents, t)
    banded = with_halo(latents)
    pa = turned(jnp.stack([pa, along_yx(pa)]))
    bz, pa, banded, t = phase(bz, pa, banded, t)
    t_in, banded_in = along_core(t[rows:]), along_core(banded)
    t = jnp.concatenate([t[:rows], t_in], axis=1)
    pa, t_in = phase(pa, t_in)
    cut = chunk_a - ROUTE_A
    own_a = jnp.concatenate([v[:cut] for v in [pb] + bz])
    own_b = jnp.concatenate([v[cut:] for v in [pb] + bz])
    near_a, near_b = along_xy(own_a), along_xy(own_b)
    az = [along_z(pa, s) for s in (1, 2, 3)]
    x = wide_cells(jnp.concatenate([banded, banded_in]))
    far_a = along_yx(jnp.stack([own_a, near_a]))
    far_b = along_yx(jnp.stack([own_b, near_b]))
    far_a, near_b, x, t, az = phase(far_a, near_b, x, t, az)
    by_a = jnp.stack([pa] + az, axis=2).reshape(2, 8 * ROUTE_A, lanes)

    def compute(own, near, far, t, *extra):
        n = t.shape[0]
        return vmem_call(
            functools.partial(routed_kernel, width, len(extra)),
            (shape(n, TAPS * channels), shape(n, 2 * cells), shape(2 * cells, n))
            + (shape(2, n // 2, lanes),) * 2,
            1,
            place,
            own,
            near,
            far,
            x,
            t,
            *extra,
            scratch=[pltpu.VMEM((TAPS, n, 128), F32), pltpu.VMEM((n, 2 * cells), BF)],
            flops=30 * 10**9,
        )

    kernel_a, student_a, error_a, keep_a, send_a = compute(own_a, near_a, far_a, t[:rows_a], by_a)
    got_a = along_yx(send_a)
    kernel_b, student_b, error_b, keep_b, send_b = compute(own_b, near_b, far_b, t[rows_a:])
    got_b = along_yx(send_b)
    got_a, send_b, error_b = phase(got_a, send_b, error_b)
    error = jnp.concatenate([error_a, error_b], axis=1)
    shifted = back_cells(with_halo(error.reshape(2, band, width, rows)))

    def back(l):
        return vmem_call(
            functools.partial(back_kernel, width, 2),
            shape(cells, channels, dtype=F32),
            0,
            kernel_a,
            kernel_b,
            shifted[:, l, :, :rows_a],
            shifted[:, l, :, rows_a:],
            flops=20 * 10**9,
        )

    got2_a = along_xy(plus(keep_a[1], got_a[1]).astype(BF))
    back_other = back(1)
    student = jnp.concatenate([student_a, student_b])
    student_in = along_core(student[:, cells:])
    got2_a, got_b, back_other, shifted, student_in = phase(
        got2_a, got_b, back_other, shifted, student_in
    )
    even = z % 2 == 0

    def outward(keep, got, got2, *counts):
        g = plus(keep[0], got[0], got2).astype(BF)
        cuts = np.cumsum([4 * count for count in counts])[:-1]
        g = [v.reshape(4, -1, lanes) for v in jnp.split(g, cuts)]
        g = jnp.concatenate(g, axis=1)
        send = jnp.where(even, jnp.stack([g[3], g[1]]), jnp.stack([g[1], g[3]]))
        return g, along_pair(send)

    g_a, pair_a = outward(keep_a, got_a, got2_a, ROUTE_A, cut)
    got2_b = along_xy(plus(keep_b[1], got_b[1]).astype(BF))
    back_own = back(0)
    got2_b, student, student_in, back_own, back_other = phase(
        got2_b, student, student_in, back_own, back_other
    )
    g_b, pair_b = outward(keep_b, got_b, got2_b, chunk_b)
    last_a = along_z(plus(g_a[2], pair_a[1]).astype(BF), 2)
    last_b = along_z(plus(g_b[2], pair_b[1]).astype(BF), 2)
    back_in = along_core(back_other)
    both = jnp.concatenate([student[:, :cells], student_in])
    out = mm(both, pick, (((0,), (0,)), ((), ()))).astype(BF).reshape(latents.shape)
    input_grad = (back_own + back_in).astype(BF).reshape(latents.shape)
    last_a, last_b, out, input_grad = phase(last_a, last_b, out, input_grad)
    news = vmem_call(
        functools.partial(adam_kernel, 1.0 / (b * lax.axis_size("dp"))),
        (shape(TAPS, per, weight.shape[1], dtype=F32),) * 3,
        1,
        place,
        by_tap(weight),
        by_tap(moment1),
        by_tap(moment2),
        g_a[0],
        pair_a[0],
        last_a,
        g_b[0],
        pair_b[0],
        last_b,
    )
    return (out, input_grad, *map(by_tap, news))


def solution(mesh):
    def per_device(latents, target, weight, moment1, moment2):
        routed = (
            mesh.shape["dp"] == 16
            and mesh.shape["rows"] == 2
            and latents.shape[0] == 1
            and weight.shape == (TAPS, 320, 40)
        )
        return (routed_device if routed else general_device)(
            latents, target, weight, moment1, moment2
        )

    cells = P("dp", "rows", None, None)
    weights = P(None, "rows", "dp")
    return jax.shard_map(
        per_device,
        mesh=mesh,
        in_specs=(cells, cells, weights, weights, weights),
        out_specs=(cells, cells, weights, weights, weights),
        check_vma=False,
    )
```

```python
import functools

import jax
import jax.numpy as jnp
import numpy as np
from jax import lax
from jax.experimental import pallas as pl
from jax.experimental.pallas import tpu as pltpu
from jax.sharding import PartitionSpec as P

BF = jnp.bfloat16
F32 = jnp.float32
NT = (((1,), (1,)), ((), ()))
NN = (((1,), (0,)), ((), ()))
VMEM_LIMIT = 28 << 20
TAPS = 9
CHUNKS = (24, 16)
ROUTE_A = 8


def mm(a, b, dims):
    return lax.dot_general(a, b, dims, preferred_element_type=F32)


def conv_student(kernel_ref, x_ref, t_ref, s_ref, e_ref, width, by_cell=None):
    wide = x_ref.shape[2]
    cells = x_ref.shape[1] - 2 * width
    for l in range(x_ref.shape[0]):
        at = slice(l * cells, (l + 1) * cells)
        total = None
        for a in range(3):
            term = mm(
                kernel_ref[:, a * wide : (a + 1) * wide],
                x_ref[l, a * width : a * width + cells, :],
                NT,
            )
            total = term if total is None else total + term
        student = total.astype(BF)
        s_ref[:, at] = student
        error = student.astype(F32) - t_ref[:, at].astype(F32)
        e_ref[:, at] = error.astype(BF)
        if by_cell is not None:
            by_cell[at, :] = error.T.astype(BF)


def tap_grad(x_ref, e_ref, tap, width):
    a, c = divmod(tap, 3)
    channels = x_ref.shape[2] // 3
    cells = x_ref.shape[1] - 2 * width
    total = None
    for l in range(x_ref.shape[0]):
        term = mm(
            e_ref[:, l * cells : (l + 1) * cells],
            x_ref[l, a * width : a * width + cells, c * channels : (c + 1) * channels],
            NN,
        )
        total = term if total is None else total + term
    return total


def plain_kernel(width, kernel_ref, x_ref, t_ref, s_ref, e_ref, g_ref):
    channels = x_ref.shape[2] // 3
    conv_student(kernel_ref, x_ref, t_ref, s_ref, e_ref, width)
    for tap in range(TAPS):
        g_ref[:, tap * channels : (tap + 1) * channels] = tap_grad(
            x_ref, e_ref, tap, width
        ).astype(BF)


def routed_kernel(width, extra, place_ref, own_ref, near_ref, far_ref, x_ref, t_ref, *refs):
    a_refs, refs = refs[:extra], refs[extra:]
    (k_ref, s_ref, e_ref, keep_ref, send_ref), refs = refs[:5], refs[5:]
    g_refs, (mid_ref, flat_ref) = refs[:extra], refs[extra:]
    first, on_core0 = place_ref[0] == 0, place_ref[1] == 0
    rows = k_ref.shape[0]
    skip = sum(a_ref.shape[1] for a_ref in a_refs) // 2
    near_y, far_y = slice(skip, rows // 2), slice(rows // 2 + skip, rows)
    low = lax.broadcasted_iota(jnp.int32, (rows, 128), 1) < 64
    spare = TAPS * 256

    def load(at):
        near, far = near_ref[:, at], far_ref[0, :, at]
        own = [own_ref[:, at], jnp.where(on_core0, far, near)]
        other = [jnp.where(on_core0, near, far), far_ref[1, :, at]]
        for a_ref in a_refs:
            own = [a_ref[0, :skip, at], own[0], a_ref[0, skip:, at], own[1]]
            other = [a_ref[1, :skip, at], other[0], a_ref[1, skip:, at], other[1]]
        own, other = jnp.concatenate(own), jnp.concatenate(other)
        return jnp.where(first, own, other), jnp.where(first, other, own)

    for tap in range(TAPS):
        left, right = load(slice(tap * 256, (tap + 1) * 256))
        k_ref[:, tap * 640 : tap * 640 + 256] = left
        k_ref[:, tap * 640 + 384 : (tap + 1) * 640] = right
    for pair in range(5):
        left, right = load(slice(spare + pair * 128, spare + (pair + 1) * 128))
        left, right = left.astype(F32), right.astype(F32)
        k_ref[:, 2 * pair * 640 + 256 : 2 * pair * 640 + 384] = jnp.where(
            low, left, pltpu.roll(right, 64, 1)
        ).astype(BF)
        if 2 * pair + 1 < TAPS:
            k_ref[:, (2 * pair + 1) * 640 + 256 : (2 * pair + 1) * 640 + 384] = jnp.where(
                low, pltpu.roll(left, 64, 1), right
            ).astype(BF)
    conv_student(k_ref, x_ref, t_ref, s_ref, flat_ref, width, e_ref)

    def put(at, left, right):
        left, right = left.astype(BF), right.astype(BF)
        own, other = jnp.where(first, left, right), jnp.where(first, right, left)
        for g_ref in g_refs:
            for i, rows_of in enumerate((own, other)):
                g_ref[i, 0, :, at] = rows_of[: near_y.start]
                g_ref[i, 1, :, at] = rows_of[near_y.stop : far_y.start]
        own_far, other_near = own[far_y], other[near_y]
        keep_ref[0, :, at] = own[near_y]
        send_ref[1, :, at] = other[far_y]
        send_ref[0, :, at] = jnp.where(on_core0, own_far, other_near)
        keep_ref[1, :, at] = jnp.where(on_core0, other_near, own_far)

    for tap in range(TAPS):
        grad = tap_grad(x_ref, flat_ref, tap, width)
        put(slice(tap * 256, (tap + 1) * 256), grad[:, :256], grad[:, 384:])
        mid_ref[tap] = grad[:, 256:384]
    for pair in range(5):
        even = mid_ref[2 * pair]
        odd = mid_ref[2 * pair + 1] if 2 * pair + 1 < TAPS else jnp.zeros_like(even)
        put(
            slice(spare + pair * 128, spare + (pair + 1) * 128),
            jnp.where(low, even, pltpu.roll(odd, 64, 1)),
            jnp.where(low, pltpu.roll(even, 64, 1), odd),
        )


def twice(half_tile):
    return jnp.concatenate([half_tile, half_tile], axis=1)


def pack_kernel(place_ref, w_ref, out_ref):
    first = place_ref[0] == 0
    low = lax.broadcasted_iota(jnp.int32, (w_ref.shape[1], 128), 1) < 64
    swap = lambda v: pltpu.roll(v, 64, 1)
    spare = []
    for tap in range(TAPS):
        t0, t1 = w_ref[tap, :, :128], w_ref[tap, :, 128:256]
        t2 = twice(w_ref[tap, :, 256:])
        r1 = swap(t1)
        out_ref[:, tap * 256 : tap * 256 + 128] = jnp.where(
            first, t0, jnp.where(low, swap(t0), r1)
        ).astype(BF)
        out_ref[:, tap * 256 + 128 : (tap + 1) * 256] = jnp.where(
            first, t1, jnp.where(low, r1, t2)
        ).astype(BF)
        spare.append(jnp.where(first, t2, jnp.where(low, t0, swap(t0))))
    spare.append(jnp.zeros_like(spare[0]))
    for pair in range(5):
        at = TAPS * 256 + pair * 128
        out_ref[:, at : at + 128] = jnp.where(low, spare[2 * pair], spare[2 * pair + 1]).astype(BF)


def adam_kernel(scale, rows, extra, place_ref, w_ref, m1_ref, m2_ref, *refs):
    parts, extras, outs = refs[:3], refs[3 : 3 + extra], refs[-3:]
    first = place_ref[0] == 0
    low = lax.broadcasted_iota(jnp.int32, (rows.stop - rows.start, 128), 1) < 64
    swap = lambda v: pltpu.roll(v, 64, 1)

    def grad(at):
        p0, p1, p2 = [ref[:, at].astype(F32) for ref in parts]
        return jnp.concatenate([(p0 + p1) + p2] + [ref[:, at] for ref in extras]) * scale

    for tap in range(TAPS):
        if tap % 2 == 0:
            spare = grad(slice(TAPS * 256 + tap * 64, TAPS * 256 + tap * 64 + 128))
            spare_swap = swap(spare)
        at_low = spare if tap % 2 == 0 else spare_swap
        left = grad(slice(tap * 256, tap * 256 + 128))
        right = grad(slice(tap * 256 + 128, (tap + 1) * 256))
        left_swap, right_swap = swap(left), swap(right)
        tiles = (
            jnp.where(first, left, jnp.where(low, at_low, left_swap)),
            jnp.where(first, right, jnp.where(low, left_swap, right_swap)),
            jnp.where(first, at_low, right_swap)[:, :64],
        )
        for tile, at in zip(tiles, (slice(0, 128), slice(128, 256), slice(256, 320))):
            new = adam(w_ref[tap, rows, at], m1_ref[tap, rows, at], m2_ref[tap, rows, at], tile)
            for out_ref, value in zip(outs, new):
                out_ref[tap, rows, at] = value


def back_kernel(width, parts, *refs):
    kernel_refs, e_refs, out_ref = refs[:parts], refs[parts : 2 * parts], refs[-1]
    channels = kernel_refs[0].shape[1] // TAPS
    cells = e_refs[0].shape[1] - 2 * width
    total = None
    for tap in range(TAPS):
        a, c = divmod(tap, 3)
        for kernel_ref, e_ref in zip(kernel_refs, e_refs):
            term = mm(
                e_ref[c, (2 - a) * width : (2 - a) * width + cells, :],
                kernel_ref[:, tap * channels : (tap + 1) * channels],
                NN,
            )
            total = term if total is None else total + term
    out_ref[...] = total


def vmem_call(kernel, outs, scalars, *args, scratch=(), flops=0):
    return pl.pallas_call(
        kernel,
        out_shape=outs,
        in_specs=[pl.BlockSpec(memory_space=pltpu.SMEM)] * scalars
        + [pl.BlockSpec(memory_space=pltpu.VMEM)] * (len(args) - scalars),
        out_specs=jax.tree.map(lambda _: pl.BlockSpec(memory_space=pltpu.VMEM), outs),
        scratch_shapes=scratch,
        cost_estimate=pl.CostEstimate(flops=flops, bytes_accessed=1 << 20, transcendentals=0),
        compiler_params=pltpu.CompilerParams(vmem_limit_bytes=VMEM_LIMIT),
    )(*args)


def shape(*dims, dtype=BF):
    return jax.ShapeDtypeStruct(dims, dtype)


def column_shift(cells, by):
    if by == 0:
        return cells
    zero = jnp.zeros_like(cells[:, :, :1])
    if by > 0:
        return jnp.concatenate([cells[:, :, 1:], zero], axis=2)
    return jnp.concatenate([zero, cells[:, :, :-1]], axis=2)


def adam(weight, moment1, moment2, grad):
    new_moment1 = 0.9 * moment1 + 0.1 * grad
    new_moment2 = 0.999 * moment2 + 0.001 * grad * grad
    new_weight = weight - 0.01 * new_moment1 / (jnp.sqrt(new_moment2) + 1e-08)
    return new_weight, new_moment1, new_moment2


def with_halo(cells):
    count = lax.axis_size("rows")
    if count == 2:
        at_top = lax.axis_index("rows") == 0
        edge = jnp.where(at_top, cells[:, -1:], cells[:, :1])
        got = lax.ppermute(edge, "rows", [(0, 1), (1, 0)])
        zero = jnp.zeros_like(got)
        return jnp.concatenate(
            [jnp.where(at_top, zero, got), cells, jnp.where(at_top, got, zero)], axis=1
        )
    up = lax.ppermute(cells[:, -1:], "rows", [(i, i + 1) for i in range(count - 1)])
    down = lax.ppermute(cells[:, :1], "rows", [(i + 1, i) for i in range(count - 1)])
    return jnp.concatenate([up, cells, down], axis=1)


def wide_cells(cells):
    b, h, w, c = cells.shape
    return jnp.concatenate([column_shift(cells, k - 1) for k in range(3)], axis=3).reshape(
        b, h * w, 3 * c
    )


def back_cells(error):
    b, h, w, n = error.shape
    return jnp.stack([column_shift(error, 1 - k) for k in range(3)]).reshape(3, b, h * w, n)


def general_device(latents, target, weight, moment1, moment2):
    b, band, width, channels = latents.shape
    cells = b * band * width
    part, outs = weight.shape[1], weight.shape[2]
    row_count = lax.axis_size("rows")
    packed = weight.astype(BF).transpose(2, 0, 1)
    gathered = lax.all_gather(packed, "dp", axis=0, tiled=True)
    kernel = lax.all_gather(gathered, "rows", axis=2, tiled=True)
    total_out = kernel.shape[0]
    kernel = kernel.reshape(total_out, TAPS * channels)
    x = wide_cells(with_halo(latents))
    t = target.reshape(cells, total_out).T
    student, error, grad = vmem_call(
        functools.partial(plain_kernel, width),
        (shape(total_out, cells), shape(total_out, cells), shape(total_out, TAPS * channels)),
        0,
        kernel,
        x,
        t,
    )
    error = error.T.reshape(b, band, width, total_out)
    shifted = back_cells(with_halo(error))
    back = [
        vmem_call(
            functools.partial(back_kernel, width, 1),
            shape(band * width, channels, dtype=F32),
            0,
            kernel,
            shifted[:, l],
        )
        for l in range(b)
    ]
    grad = grad.astype(F32).reshape(total_out, TAPS, row_count, part).transpose(2, 0, 1, 3)
    grad = lax.psum_scatter(grad, "rows", scatter_dimension=0, tiled=True)[0]
    grad = lax.psum_scatter(grad, "dp", scatter_dimension=0, tiled=True)
    grad = grad.transpose(1, 2, 0) / F32(b * lax.axis_size("dp"))
    return (
        student.T.reshape(latents.shape),
        jnp.stack(back).astype(BF).reshape(latents.shape),
        *adam(weight, moment1, moment2, grad),
    )


def hop(pairs_of):
    pairs = []
    for i in range(32):
        z, y, core, x = i // 8, i // 4 % 2, i // 2 % 2, i % 2
        z, y, core, x = pairs_of(z, y, core, x)
        pairs.append((i, ((z % 4 * 2 + y) * 2 + core) * 2 + x))
    return lambda v: lax.ppermute(v, ("dp", "rows"), pairs)


def phase(*values):
    return lax.optimization_barrier(values)


def routed_device(latents, target, weight, moment1, moment2):
    b, band, width, channels = latents.shape
    cells = band * width
    index = lax.axis_index("dp")
    core, y, z = index % 2, (index // 2) % 2, index // 4
    half = lax.axis_index("rows")
    along_core = hop(lambda z, y, core, x: (z, y, 1 - core, x))
    along_xy = hop(lambda z, y, core, x: (z, y ^ core, core, x ^ 1 ^ core))
    along_yx = hop(lambda z, y, core, x: (z, y ^ 1 ^ core, core, x ^ core))
    along_z = lambda v, s: hop(lambda z, y, core, x: (z + s, y, core, x))(v)
    along_pair = hop(lambda z, y, core, x: (z ^ 1, y, core, x))
    lanes = TAPS * 256 + 640

    place = jnp.stack([half, core]).astype(jnp.int32)
    by_tap = lambda v: v.transpose(0, 2, 1)
    per = weight.shape[2]
    piece = vmem_call(pack_kernel, shape(per, lanes), 1, place, by_tap(weight))
    piece, latents, target = phase(piece, latents, target)

    def turned(v):
        return jnp.where(core == 0, v.swapaxes(0, 1), v)

    chunk_a, chunk_b = CHUNKS
    grids = []
    cut = chunk_a - ROUTE_A
    for spans in (((chunk_b + cut, ROUTE_A), (chunk_b, cut)), ((0, chunk_b),)):
        for dist_y in range(2):
            for begin, count in spans:
                dist_z, within = np.indices((4, count)).reshape(2, -1)
                grids.append(np.stack([np.full_like(dist_z, dist_y), dist_z, begin + within]))
    dist_y, dist_z, within = np.concatenate(grids, axis=1).astype(np.int32)
    block = ((z - dist_z) % 4) * 4 + (y ^ dist_y) * 2
    everything = jnp.arange(channels, dtype=jnp.int32)
    pick_own = ((block + core) * per + within)[:, None] == everything[None, :]
    pick_other = ((block + 1 - core) * per + within)[:, None] == everything[None, :]
    pick = jnp.concatenate([pick_own, pick_other]).astype(BF)
    rows = within.shape[0]
    rows_a = 8 * chunk_a

    def plus(*terms):
        total = terms[0].astype(F32)
        for term in terms[1:]:
            total = total + term.astype(F32)
        return total

    pa, pb = piece[chunk_b + cut :], piece[: chunk_b + cut]
    bz = [along_z(pb, s) for s in (1, 2, 3)]
    pa = jnp.stack([pa, along_xy(pa)])
    t = mm(pick, target.reshape(cells, channels), NT).astype(BF)
    pa, latents, t = phase(pa, latents, t)
    banded = with_halo(latents)
    pa = turned(jnp.stack([pa, along_yx(pa)]))
    bz, pa, banded, t = phase(bz, pa, banded, t)
    t_in = along_core(t[rows:])
    t = jnp.concatenate([t[:rows], t_in], axis=1)
    pa, t_in = phase(pa, t_in)
    own_a = jnp.concatenate([v[chunk_b:] for v in [pb] + bz])
    own_b = jnp.concatenate([v[:chunk_b] for v in [pb] + bz])
    near_a, near_b = along_xy(own_a), along_xy(own_b)
    az = [along_z(pa, s) for s in (1, 2, 3)]
    near_a, banded = phase(near_a, banded)
    x = wide_cells(jnp.concatenate([banded, along_core(banded)]))
    far_a = along_yx(jnp.stack([own_a, near_a]))
    far_b = along_yx(jnp.stack([own_b, near_b]))
    far_a, near_b, x, t, az = phase(far_a, near_b, x, t, az)
    by_a = jnp.stack([pa] + az, axis=2).reshape(2, 8 * ROUTE_A, lanes)

    def compute(own, near, far, t, *extra):
        n = t.shape[0]
        return vmem_call(
            functools.partial(routed_kernel, width, len(extra)),
            (shape(n, TAPS * channels), shape(n, 2 * cells), shape(2 * cells, n))
            + (shape(2, own.shape[0], lanes),) * 2
            + tuple(shape(2, 2, v.shape[1] // 2, lanes) for v in extra),
            1,
            place,
            own,
            near,
            far,
            x,
            t,
            *extra,
            scratch=[pltpu.VMEM((TAPS, n, 128), F32), pltpu.VMEM((n, 2 * cells), BF)],
            flops=30 * 10**9,
        )

    kernel_a, student_a, error_a, keep_a, send_a, ga = compute(
        own_a, near_a, far_a, t[:rows_a], by_a
    )
    got_a = along_yx(send_a)
    even = z % 2 == 0

    def to_pair(g):
        return along_pair(jnp.where(even, jnp.stack([g[3], g[1]]), jnp.stack([g[1], g[3]])))

    ga = ga.reshape(2, 2, 4, ROUTE_A, lanes).transpose(2, 0, 1, 3, 4)
    pair_ga = to_pair(ga)
    kernel_b, student_b, error_b, keep_b, send_b = compute(own_b, near_b, far_b, t[rows_a:])
    got_b = along_yx(send_b)
    got_a, send_b, error_b, pair_ga = phase(got_a, send_b, error_b, pair_ga)
    last_ga = along_z(plus(ga[2], pair_ga[1]).astype(BF), 2)
    error = jnp.concatenate([error_a, error_b], axis=1)
    shifted = back_cells(with_halo(error.reshape(2, band, width, rows)))

    def back(l):
        return vmem_call(
            functools.partial(back_kernel, width, 2),
            shape(cells, channels, dtype=F32),
            0,
            kernel_a,
            kernel_b,
            shifted[:, l, :, :rows_a],
            shifted[:, l, :, rows_a:],
            flops=20 * 10**9,
        )

    got2_a = along_xy(plus(keep_a[1], got_a[1]).astype(BF))
    back_other = back(1)
    student = jnp.concatenate([student_a, student_b])
    student_in = along_core(student[:, cells:])
    got2_a, got_b, back_other, shifted, student_in, last_ga = phase(
        got2_a, got_b, back_other, shifted, student_in, last_ga
    )

    def second_sum(keep, got, got2):
        return plus(keep[0], got[0], got2).astype(BF).reshape(4, -1, lanes)

    g_a = second_sum(keep_a, got_a, got2_a)
    pair_a = to_pair(g_a)
    got2_b = along_xy(plus(keep_b[1], got_b[1]).astype(BF))
    ga = turned(plus(ga[0], pair_ga[0], last_ga))
    ga = plus(ga[0], along_yx(ga[1].astype(BF)))
    back_own = back(0)
    got2_b, student, student_in, back_own, back_other, ga = phase(
        got2_b, student, student_in, back_own, back_other, ga
    )
    g_b = second_sum(keep_b, got_b, got2_b)
    pair_b = to_pair(g_b)
    last_a = along_z(plus(g_a[2], pair_a[1]).astype(BF), 2)
    last_b = along_z(plus(g_b[2], pair_b[1]).astype(BF), 2)
    ga = plus(ga[0], along_xy(ga[1].astype(BF)))
    back_in = along_core(back_other)
    both = jnp.concatenate([student[:, :cells], student_in])
    out = mm(both, pick, (((0,), (0,)), ((), ()))).astype(BF).reshape(latents.shape)
    input_grad = (back_own + back_in).astype(BF).reshape(latents.shape)
    last_a, ga, out, input_grad = phase(last_a, ga, out, input_grad)

    scale = 1.0 / (b * lax.axis_size("dp"))
    states = [by_tap(v) for v in (weight, moment1, moment2)]
    whole = (shape(TAPS, per, weight.shape[1], dtype=F32),) * 3
    news = vmem_call(
        functools.partial(adam_kernel, scale, slice(chunk_b, per), 1),
        whole,
        1,
        place,
        *states,
        g_a[0],
        pair_a[0],
        last_a,
        ga,
    )
    last_b, news = phase(last_b, news)
    some = pl.BlockSpec((TAPS, chunk_b, weight.shape[1]), lambda i: (0, 0, 0))
    full = pl.BlockSpec((chunk_b, lanes), lambda i: (0, 0))
    news = pl.pallas_call(
        functools.partial(adam_kernel, scale, slice(0, chunk_b), 0),
        out_shape=whole,
        grid=(1,),
        in_specs=[pl.BlockSpec(memory_space=pltpu.SMEM)]
        + [some] * 3
        + [full] * 3
        + [pl.BlockSpec(memory_space=pl.ANY)] * 3,
        out_specs=(some,) * 3,
        input_output_aliases={7: 0, 8: 1, 9: 2},
        compiler_params=pltpu.CompilerParams(vmem_limit_bytes=VMEM_LIMIT),
    )(place, *states, g_b[0], pair_b[0], last_b, *news)
    return (out, input_grad, *map(by_tap, news))


def solution(mesh):
    def per_device(latents, target, weight, moment1, moment2):
        routed = (
            mesh.shape["dp"] == 16
            and mesh.shape["rows"] == 2
            and latents.shape[0] == 1
            and weight.shape == (TAPS, 320, 40)
        )
        return (routed_device if routed else general_device)(
            latents, target, weight, moment1, moment2
        )

    cells = P("dp", "rows", None, None)
    weights = P(None, "rows", "dp")
    return jax.shard_map(
        per_device,
        mesh=mesh,
        in_specs=(cells, cells, weights, weights, weights),
        out_specs=(cells, cells, weights, weights, weights),
        check_vma=False,
    )
```

```python
import functools

import jax
import jax.numpy as jnp
import numpy as np
from jax import lax
from jax.experimental import pallas as pl
from jax.experimental.pallas import tpu as pltpu
from jax.sharding import PartitionSpec as P

BF = jnp.bfloat16
F32 = jnp.float32
NT = (((1,), (1,)), ((), ()))
NN = (((1,), (0,)), ((), ()))
VMEM_LIMIT = 22 << 20
TAPS = 9
CHUNKS = (24, 16)
ROUTE_A = 8


def mm(a, b, dims):
    return lax.dot_general(a, b, dims, preferred_element_type=F32)


def conv_student(kernel_ref, x_ref, t_ref, s_ref, e_ref, width, by_cell=None):
    wide = x_ref.shape[2]
    cells = x_ref.shape[1] - 2 * width
    for l in range(x_ref.shape[0]):
        at = slice(l * cells, (l + 1) * cells)
        total = None
        for a in range(3):
            term = mm(
                kernel_ref[:, a * wide : (a + 1) * wide],
                x_ref[l, a * width : a * width + cells, :],
                NT,
            )
            total = term if total is None else total + term
        student = total.astype(BF)
        s_ref[:, at] = student
        error = student.astype(F32) - t_ref[:, at].astype(F32)
        e_ref[:, at] = error.astype(BF)
        if by_cell is not None:
            by_cell[at, :] = error.T.astype(BF)


def tap_grad(x_ref, e_ref, tap, width):
    a, c = divmod(tap, 3)
    channels = x_ref.shape[2] // 3
    cells = x_ref.shape[1] - 2 * width
    total = None
    for l in range(x_ref.shape[0]):
        term = mm(
            e_ref[:, l * cells : (l + 1) * cells],
            x_ref[l, a * width : a * width + cells, c * channels : (c + 1) * channels],
            NN,
        )
        total = term if total is None else total + term
    return total


def plain_kernel(width, kernel_ref, x_ref, t_ref, s_ref, e_ref, g_ref):
    channels = x_ref.shape[2] // 3
    conv_student(kernel_ref, x_ref, t_ref, s_ref, e_ref, width)
    for tap in range(TAPS):
        g_ref[:, tap * channels : (tap + 1) * channels] = tap_grad(
            x_ref, e_ref, tap, width
        ).astype(BF)


def routed_kernel(width, extra, place_ref, own_ref, near_ref, far_ref, x_ref, t_ref, *refs):
    a_refs, refs = refs[:extra], refs[extra:]
    (k_ref, s_ref, e_ref, keep_ref, send_ref), refs = refs[:5], refs[5:]
    g_refs, (mid_ref, flat_ref) = refs[:extra], refs[extra:]
    first, on_core0 = place_ref[0] == 0, place_ref[1] == 0
    rows = k_ref.shape[0]
    skip = sum(a_ref.shape[1] for a_ref in a_refs) // 2
    near_y, far_y = slice(skip, rows // 2), slice(rows // 2 + skip, rows)
    low = lax.broadcasted_iota(jnp.int32, (rows, 128), 1) < 64
    spare = TAPS * 256

    def load(at):
        near, far = near_ref[:, at], far_ref[0, :, at]
        own = [own_ref[:, at], jnp.where(on_core0, far, near)]
        other = [jnp.where(on_core0, near, far), far_ref[1, :, at]]
        for a_ref in a_refs:
            own = [a_ref[0, :skip, at], own[0], a_ref[0, skip:, at], own[1]]
            other = [a_ref[1, :skip, at], other[0], a_ref[1, skip:, at], other[1]]
        own, other = jnp.concatenate(own), jnp.concatenate(other)
        return jnp.where(first, own, other), jnp.where(first, other, own)

    for tap in range(TAPS):
        left, right = load(slice(tap * 256, (tap + 1) * 256))
        k_ref[:, tap * 640 : tap * 640 + 256] = left
        k_ref[:, tap * 640 + 384 : (tap + 1) * 640] = right
    for pair in range(5):
        left, right = load(slice(spare + pair * 128, spare + (pair + 1) * 128))
        left, right = left.astype(F32), right.astype(F32)
        k_ref[:, 2 * pair * 640 + 256 : 2 * pair * 640 + 384] = jnp.where(
            low, left, pltpu.roll(right, 64, 1)
        ).astype(BF)
        if 2 * pair + 1 < TAPS:
            k_ref[:, (2 * pair + 1) * 640 + 256 : (2 * pair + 1) * 640 + 384] = jnp.where(
                low, pltpu.roll(left, 64, 1), right
            ).astype(BF)
    conv_student(k_ref, x_ref, t_ref, s_ref, flat_ref, width, e_ref)

    def put(at, left, right):
        left, right = left.astype(BF), right.astype(BF)
        own, other = jnp.where(first, left, right), jnp.where(first, right, left)
        for g_ref in g_refs:
            for i, rows_of in enumerate((own, other)):
                g_ref[i, 0, :, at] = rows_of[: near_y.start]
                g_ref[i, 1, :, at] = rows_of[near_y.stop : far_y.start]
        own_far, other_near = own[far_y], other[near_y]
        keep_ref[0, :, at] = own[near_y]
        send_ref[1, :, at] = other[far_y]
        send_ref[0, :, at] = jnp.where(on_core0, own_far, other_near)
        keep_ref[1, :, at] = jnp.where(on_core0, other_near, own_far)

    for tap in range(TAPS):
        grad = tap_grad(x_ref, flat_ref, tap, width)
        put(slice(tap * 256, (tap + 1) * 256), grad[:, :256], grad[:, 384:])
        mid_ref[tap] = grad[:, 256:384]
    for pair in range(5):
        even = mid_ref[2 * pair]
        odd = mid_ref[2 * pair + 1] if 2 * pair + 1 < TAPS else jnp.zeros_like(even)
        put(
            slice(spare + pair * 128, spare + (pair + 1) * 128),
            jnp.where(low, even, pltpu.roll(odd, 64, 1)),
            jnp.where(low, pltpu.roll(even, 64, 1), odd),
        )


def twice(half_tile):
    return jnp.concatenate([half_tile, half_tile], axis=1)


def pack_kernel(place_ref, w_ref, out_ref):
    first = place_ref[0] == 0
    low = lax.broadcasted_iota(jnp.int32, (w_ref.shape[1], 128), 1) < 64
    swap = lambda v: pltpu.roll(v, 64, 1)
    spare = []
    for tap in range(TAPS):
        t0, t1 = w_ref[tap, :, :128], w_ref[tap, :, 128:256]
        t2 = twice(w_ref[tap, :, 256:])
        r1 = swap(t1)
        out_ref[:, tap * 256 : tap * 256 + 128] = jnp.where(
            first, t0, jnp.where(low, swap(t0), r1)
        ).astype(BF)
        out_ref[:, tap * 256 + 128 : (tap + 1) * 256] = jnp.where(
            first, t1, jnp.where(low, r1, t2)
        ).astype(BF)
        spare.append(jnp.where(first, t2, jnp.where(low, t0, swap(t0))))
    spare.append(jnp.zeros_like(spare[0]))
    for pair in range(5):
        at = TAPS * 256 + pair * 128
        out_ref[:, at : at + 128] = jnp.where(low, spare[2 * pair], spare[2 * pair + 1]).astype(BF)


def adam_kernel(scale, rows, extra, place_ref, w_ref, m1_ref, m2_ref, *refs):
    parts, extras, outs = refs[:3], refs[3 : 3 + extra], refs[-3:]
    first = place_ref[0] == 0
    low = lax.broadcasted_iota(jnp.int32, (rows.stop - rows.start, 128), 1) < 64
    swap = lambda v: pltpu.roll(v, 64, 1)

    def grad(at):
        p0, p1, p2 = [ref[:, at].astype(F32) for ref in parts]
        return jnp.concatenate([(p0 + p1) + p2] + [ref[:, at] for ref in extras]) * scale

    for tap in range(TAPS):
        if tap % 2 == 0:
            spare = grad(slice(TAPS * 256 + tap * 64, TAPS * 256 + tap * 64 + 128))
            spare_swap = swap(spare)
        at_low = spare if tap % 2 == 0 else spare_swap
        left = grad(slice(tap * 256, tap * 256 + 128))
        right = grad(slice(tap * 256 + 128, (tap + 1) * 256))
        left_swap, right_swap = swap(left), swap(right)
        tiles = (
            jnp.where(first, left, jnp.where(low, at_low, left_swap)),
            jnp.where(first, right, jnp.where(low, left_swap, right_swap)),
            jnp.where(first, at_low, right_swap)[:, :64],
        )
        for tile, at in zip(tiles, (slice(0, 128), slice(128, 256), slice(256, 320))):
            new = adam(w_ref[tap, rows, at], m1_ref[tap, rows, at], m2_ref[tap, rows, at], tile)
            for out_ref, value in zip(outs, new):
                out_ref[tap, rows, at] = value


def back_kernel(width, parts, *refs):
    kernel_refs, e_refs, out_ref = refs[:parts], refs[parts : 2 * parts], refs[-1]
    channels = kernel_refs[0].shape[1] // TAPS
    cells = e_refs[0].shape[1] - 2 * width
    total = None
    for tap in range(TAPS):
        a, c = divmod(tap, 3)
        for kernel_ref, e_ref in zip(kernel_refs, e_refs):
            term = mm(
                e_ref[c, (2 - a) * width : (2 - a) * width + cells, :],
                kernel_ref[:, tap * channels : (tap + 1) * channels],
                NN,
            )
            total = term if total is None else total + term
    out_ref[...] = total


def vmem_call(kernel, outs, scalars, *args, scratch=(), flops=0):
    return pl.pallas_call(
        kernel,
        out_shape=outs,
        in_specs=[pl.BlockSpec(memory_space=pltpu.SMEM)] * scalars
        + [pl.BlockSpec(memory_space=pltpu.VMEM)] * (len(args) - scalars),
        out_specs=jax.tree.map(lambda _: pl.BlockSpec(memory_space=pltpu.VMEM), outs),
        scratch_shapes=scratch,
        cost_estimate=pl.CostEstimate(flops=flops, bytes_accessed=1 << 20, transcendentals=0),
        compiler_params=pltpu.CompilerParams(vmem_limit_bytes=VMEM_LIMIT),
    )(*args)


def shape(*dims, dtype=BF):
    return jax.ShapeDtypeStruct(dims, dtype)


def column_shift(cells, by):
    if by == 0:
        return cells
    zero = jnp.zeros_like(cells[:, :, :1])
    if by > 0:
        return jnp.concatenate([cells[:, :, 1:], zero], axis=2)
    return jnp.concatenate([zero, cells[:, :, :-1]], axis=2)


def adam(weight, moment1, moment2, grad):
    new_moment1 = 0.9 * moment1 + 0.1 * grad
    new_moment2 = 0.999 * moment2 + 0.001 * grad * grad
    new_weight = weight - 0.01 * new_moment1 / (jnp.sqrt(new_moment2) + 1e-08)
    return new_weight, new_moment1, new_moment2


def with_halo(cells):
    count = lax.axis_size("rows")
    if count == 2:
        at_top = lax.axis_index("rows") == 0
        edge = jnp.where(at_top, cells[:, -1:], cells[:, :1])
        got = lax.ppermute(edge, "rows", [(0, 1), (1, 0)])
        zero = jnp.zeros_like(got)
        return jnp.concatenate(
            [jnp.where(at_top, zero, got), cells, jnp.where(at_top, got, zero)], axis=1
        )
    up = lax.ppermute(cells[:, -1:], "rows", [(i, i + 1) for i in range(count - 1)])
    down = lax.ppermute(cells[:, :1], "rows", [(i + 1, i) for i in range(count - 1)])
    return jnp.concatenate([up, cells, down], axis=1)


def wide_cells(cells):
    b, h, w, c = cells.shape
    return jnp.concatenate([column_shift(cells, k - 1) for k in range(3)], axis=3).reshape(
        b, h * w, 3 * c
    )


def back_cells(error):
    b, h, w, n = error.shape
    return jnp.stack([column_shift(error, 1 - k) for k in range(3)]).reshape(3, b, h * w, n)


def general_device(latents, target, weight, moment1, moment2):
    b, band, width, channels = latents.shape
    cells = b * band * width
    part, outs = weight.shape[1], weight.shape[2]
    row_count = lax.axis_size("rows")
    packed = weight.astype(BF).transpose(2, 0, 1)
    gathered = lax.all_gather(packed, "dp", axis=0, tiled=True)
    kernel = lax.all_gather(gathered, "rows", axis=2, tiled=True)
    total_out = kernel.shape[0]
    kernel = kernel.reshape(total_out, TAPS * channels)
    x = wide_cells(with_halo(latents))
    t = target.reshape(cells, total_out).T
    student, error, grad = vmem_call(
        functools.partial(plain_kernel, width),
        (shape(total_out, cells), shape(total_out, cells), shape(total_out, TAPS * channels)),
        0,
        kernel,
        x,
        t,
    )
    error = error.T.reshape(b, band, width, total_out)
    shifted = back_cells(with_halo(error))
    back = [
        vmem_call(
            functools.partial(back_kernel, width, 1),
            shape(band * width, channels, dtype=F32),
            0,
            kernel,
            shifted[:, l],
        )
        for l in range(b)
    ]
    grad = grad.astype(F32).reshape(total_out, TAPS, row_count, part).transpose(2, 0, 1, 3)
    grad = lax.psum_scatter(grad, "rows", scatter_dimension=0, tiled=True)[0]
    grad = lax.psum_scatter(grad, "dp", scatter_dimension=0, tiled=True)
    grad = grad.transpose(1, 2, 0) / F32(b * lax.axis_size("dp"))
    return (
        student.T.reshape(latents.shape),
        jnp.stack(back).astype(BF).reshape(latents.shape),
        *adam(weight, moment1, moment2, grad),
    )


def hop(pairs_of):
    pairs = []
    for i in range(32):
        z, y, core, x = i // 8, i // 4 % 2, i // 2 % 2, i % 2
        z, y, core, x = pairs_of(z, y, core, x)
        pairs.append((i, ((z % 4 * 2 + y) * 2 + core) * 2 + x))
    return lambda v: lax.ppermute(v, ("dp", "rows"), pairs)


def phase(*values):
    return lax.optimization_barrier(values)


def routed_device(latents, target, weight, moment1, moment2):
    b, band, width, channels = latents.shape
    cells = band * width
    index = lax.axis_index("dp")
    core, y, z = index % 2, (index // 2) % 2, index // 4
    half = lax.axis_index("rows")
    along_core = hop(lambda z, y, core, x: (z, y, 1 - core, x))
    along_xy = hop(lambda z, y, core, x: (z, y ^ core, core, x ^ 1 ^ core))
    along_yx = hop(lambda z, y, core, x: (z, y ^ 1 ^ core, core, x ^ core))
    along_z = lambda v, s: hop(lambda z, y, core, x: (z + s, y, core, x))(v)
    along_pair = hop(lambda z, y, core, x: (z ^ 1, y, core, x))
    lanes = TAPS * 256 + 640

    place = jnp.stack([half, core]).astype(jnp.int32)
    by_tap = lambda v: v.transpose(0, 2, 1)
    per = weight.shape[2]
    piece = vmem_call(pack_kernel, shape(per, lanes), 1, place, by_tap(weight))
    piece, latents, target = phase(piece, latents, target)

    def turned(v):
        return jnp.where(core == 0, v.swapaxes(0, 1), v)

    chunk_a, chunk_b = CHUNKS
    grids = []
    cut = chunk_a - ROUTE_A
    for spans in (((chunk_b + cut, ROUTE_A), (chunk_b, cut)), ((0, chunk_b),)):
        for dist_y in range(2):
            for begin, count in spans:
                dist_z, within = np.indices((4, count)).reshape(2, -1)
                grids.append(np.stack([np.full_like(dist_z, dist_y), dist_z, begin + within]))
    dist_y, dist_z, within = np.concatenate(grids, axis=1).astype(np.int32)
    block = ((z - dist_z) % 4) * 4 + (y ^ dist_y) * 2
    everything = jnp.arange(channels, dtype=jnp.int32)
    pick_own = ((block + core) * per + within)[:, None] == everything[None, :]
    pick_other = ((block + 1 - core) * per + within)[:, None] == everything[None, :]
    pick = jnp.concatenate([pick_own, pick_other]).astype(BF)
    rows = within.shape[0]
    rows_a = 8 * chunk_a

    def plus(*terms):
        total = terms[0].astype(F32)
        for term in terms[1:]:
            total = total + term.astype(F32)
        return total

    pa, pb = piece[chunk_b + cut :], piece[: chunk_b + cut]
    bz = [along_z(pb, s) for s in (1, 2, 3)]
    pa = jnp.stack([pa, along_xy(pa)])
    t = mm(pick, target.reshape(cells, channels), NT).astype(BF)
    pa, latents, t = phase(pa, latents, t)
    banded = with_halo(latents)
    pa = turned(jnp.stack([pa, along_yx(pa)]))
    bz, pa, banded, t = phase(bz, pa, banded, t)
    t_in = along_core(t[rows:])
    t = jnp.concatenate([t[:rows], t_in], axis=1)
    pa, t_in = phase(pa, t_in)
    own_a = jnp.concatenate([v[chunk_b:] for v in [pb] + bz])
    own_b = jnp.concatenate([v[:chunk_b] for v in [pb] + bz])
    near_a, near_b = along_xy(own_a), along_xy(own_b)
    az = [along_z(pa, s) for s in (1, 2, 3)]
    near_a, banded = phase(near_a, banded)
    x = wide_cells(jnp.concatenate([banded, along_core(banded)]))
    far_a = along_yx(jnp.stack([own_a, near_a]))
    far_b = along_yx(jnp.stack([own_b, near_b]))
    far_a, near_b, x, t, az = phase(far_a, near_b, x, t, az)
    by_a = jnp.stack([pa] + az, axis=2).reshape(2, 8 * ROUTE_A, lanes)

    def compute(own, near, far, t, *extra):
        n = t.shape[0]
        return vmem_call(
            functools.partial(routed_kernel, width, len(extra)),
            (shape(n, TAPS * channels), shape(n, 2 * cells), shape(2 * cells, n))
            + (shape(2, own.shape[0], lanes),) * 2
            + tuple(shape(2, 2, v.shape[1] // 2, lanes) for v in extra),
            1,
            place,
            own,
            near,
            far,
            x,
            t,
            *extra,
            scratch=[pltpu.VMEM((TAPS, n, 128), F32), pltpu.VMEM((n, 2 * cells), BF)],
            flops=30 * 10**9,
        )

    kernel_a, student_a, error_a, keep_a, send_a, ga = compute(
        own_a, near_a, far_a, t[:rows_a], by_a
    )
    got_a = along_yx(send_a)
    even = z % 2 == 0

    def to_pair(g):
        return along_pair(jnp.where(even, jnp.stack([g[3], g[1]]), jnp.stack([g[1], g[3]])))

    ga = ga.reshape(2, 2, 4, ROUTE_A, lanes).transpose(2, 0, 1, 3, 4)
    pair_ga = to_pair(ga)
    kernel_b, student_b, error_b, keep_b, send_b = compute(own_b, near_b, far_b, t[rows_a:])
    got_b = along_yx(send_b)
    got_a, send_b, error_b, pair_ga = phase(got_a, send_b, error_b, pair_ga)
    last_ga = along_z(plus(ga[2], pair_ga[1]).astype(BF), 2)
    error = jnp.concatenate([error_a, error_b], axis=1)
    shifted = back_cells(with_halo(error.reshape(2, band, width, rows)))

    def back(l):
        return vmem_call(
            functools.partial(back_kernel, width, 2),
            shape(cells, channels, dtype=F32),
            0,
            kernel_a,
            kernel_b,
            shifted[:, l, :, :rows_a],
            shifted[:, l, :, rows_a:],
            flops=20 * 10**9,
        )

    got2_a = along_xy(plus(keep_a[1], got_a[1]).astype(BF))
    back_other = back(1)
    student = jnp.concatenate([student_a, student_b])
    student_in = along_core(student[:, cells:])
    got2_a, got_b, back_other, shifted, student_in, last_ga = phase(
        got2_a, got_b, back_other, shifted, student_in, last_ga
    )

    def second_sum(keep, got, got2):
        return plus(keep[0], got[0], got2).astype(BF).reshape(4, -1, lanes)

    g_a = second_sum(keep_a, got_a, got2_a)
    pair_a = to_pair(g_a)
    got2_b = along_xy(plus(keep_b[1], got_b[1]).astype(BF))
    ga = turned(plus(ga[0], pair_ga[0], last_ga))
    ga = plus(ga[0], along_yx(ga[1].astype(BF)))
    back_own = back(0)
    got2_b, student, student_in, back_own, back_other, ga = phase(
        got2_b, student, student_in, back_own, back_other, ga
    )
    g_b = second_sum(keep_b, got_b, got2_b)
    pair_b = to_pair(g_b)
    last_a = along_z(plus(g_a[2], pair_a[1]).astype(BF), 2)
    last_b = along_z(plus(g_b[2], pair_b[1]).astype(BF), 2)
    ga = plus(ga[0], along_xy(ga[1].astype(BF)))
    back_in = along_core(back_other)
    both = jnp.concatenate([student[:, :cells], student_in])
    out = mm(both, pick, (((0,), (0,)), ((), ()))).astype(BF).reshape(latents.shape)
    input_grad = (back_own + back_in).astype(BF).reshape(latents.shape)
    last_a, ga, out, input_grad = phase(last_a, ga, out, input_grad)

    scale = 1.0 / (b * lax.axis_size("dp"))
    states = [by_tap(v) for v in (weight, moment1, moment2)]
    whole = (shape(TAPS, per, weight.shape[1], dtype=F32),) * 3
    news = vmem_call(
        functools.partial(adam_kernel, scale, slice(chunk_b, per), 1),
        whole,
        1,
        place,
        *states,
        g_a[0],
        pair_a[0],
        last_a,
        ga,
    )
    last_b, news = phase(last_b, news)
    some = pl.BlockSpec((TAPS, chunk_b, weight.shape[1]), lambda i: (0, 0, 0))
    full = pl.BlockSpec((chunk_b, lanes), lambda i: (0, 0))
    news = pl.pallas_call(
        functools.partial(adam_kernel, scale, slice(0, chunk_b), 0),
        out_shape=whole,
        grid=(1,),
        in_specs=[pl.BlockSpec(memory_space=pltpu.SMEM)]
        + [some] * 3
        + [full] * 3
        + [pl.BlockSpec(memory_space=pl.ANY)] * 3,
        out_specs=(some,) * 3,
        input_output_aliases={7: 0, 8: 1, 9: 2},
        compiler_params=pltpu.CompilerParams(vmem_limit_bytes=VMEM_LIMIT),
    )(place, *states, g_b[0], pair_b[0], last_b, *news)
    return (out, input_grad, *map(by_tap, news))


def solution(mesh):
    def per_device(latents, target, weight, moment1, moment2):
        routed = (
            mesh.shape["dp"] == 16
            and mesh.shape["rows"] == 2
            and latents.shape[0] == 1
            and weight.shape == (TAPS, 320, 40)
        )
        return (routed_device if routed else general_device)(
            latents, target, weight, moment1, moment2
        )

    cells = P("dp", "rows", None, None)
    weights = P(None, "rows", "dp")
    return jax.shard_map(
        per_device,
        mesh=mesh,
        in_specs=(cells, cells, weights, weights, weights),
        out_specs=(cells, cells, weights, weights, weights),
        check_vma=False,
    )
```
